32 devices in a mesh: col: 4 (over x, core), row: 8 (over z, y).
Axes of the slice: x: 2, y: 2, z: 4, core: 2. Of those that a mesh axis runs over, the one named last changes fastest.
Arguments:
- slip: bfloat16 [64, 32768], P(None, ('col', 'row')), may hold values from -6 to 6
- lowrank_u: bfloat16 [4, 8192, 2048], P(None, 'row', 'col'), may hold values from -0.5 to 0.5
- lowrank_v: bfloat16 [4, 64, 2048, 128], P(None, 'col', 'row'), may hold values from -0.09375 to 0.09375
- ranks: int32 [4, 64, 64], P(None, 'row', 'col'), may hold values from 8 to 32
- near_slot: int32 [4, 64, 8], P(None, 'row', 'col'), may hold values from 0 to 15, as said below
- near_blocks: bfloat16 [4, 8192, 1024], P(None, 'row', 'col'), may hold values from -0.09375 to 0.09375
- velocity: float32 [64, 8192], P(None, ('col', 'row')), may hold values from 0.3 to 3
- theta: float32 [64, 8192], P(None, ('col', 'row')), may hold values from 0.3 to 3
- a_sigma: float32 [8192], P(('col', 'row')), may hold values from 0.5 to 2
- b_sigma: float32 [8192], P(('col', 'row')), may hold values from 0.5 to 2
Outputs:
- stress_rate: float32 [64, 8192], P(None, ('col', 'row'))
- accel: float32 [64, 8192], P(None, ('col', 'row'))
The draws below stay inside these ranges and needn't reach their ends.
Inputs may be any that keep to these rules, and one draw needn't show every extreme that they name: `near_slot`: for each section, source block and receiver group, the 2 entries are distinct receiver blocks of that group. `ranks`: ranks of near-field blocks are not used.
All inputs are finite; a program needn't handle non-finite values.
Results may differ from the reference program's by a relative error of at most 0.002.
Values may be sent and summed in bfloat16 or wider, within the bound.
No kernel may reach another device: no remote copies, remote signals or barrier semaphores. Data moves between devices by JAX's collectives and lax.ppermute only.
A program may use at most 64 MiB of HBM per device.

```python
import math
import jax
import jax.numpy as jnp
from jax import lax

M = 64
BLK = 128
KMAX = 32
NEAR = 2
CB = 8
RB = 16
NC = 32768
GC = 8192
NR = 8192
N_COL = 4
N_ROW = 8


def draw_near_slot(key, part):
    total_rows = N_COL * N_ROW * CB * N_COL
    keys = jax.random.split(jax.random.fold_in(key, 17), total_rows)
    picks = jax.vmap(lambda single: jax.random.permutation(single, RB)[:NEAR])(keys)
    return picks.reshape(N_COL, N_ROW * CB, N_COL * NEAR).astype(jnp.int32)


def plant(values, key, least, largest):
    spot = [jax.random.randint(jax.random.fold_in(key, axis), (), 0, length) for axis, length in enumerate(values.shape)]
    widest = values.shape.index(max(values.shape))
    next_to = spot[:widest] + [(spot[widest] + 1) % values.shape[widest]] + spot[widest + 1:]
    return values.at[tuple(spot)].set(least).at[tuple(next_to)].set(largest)


def strengthened(values, rng, source, target, shards_of, factor):
    owner, partner = [(jnp.arange(values.shape[axis_at]) // (values.shape[axis_at] // shards_of)).reshape([-1 if axis == axis_at else 1 for axis in range(values.ndim)]) for axis_at in (source, target)]
    chosen = jax.random.permutation(rng, shards_of)[partner]
    strong = (owner == chosen) | (owner == (partner + shards_of // 2) % shards_of)
    return jnp.where(strong, factor * values, values)


def block_scale(key, extent, shards, least, largest):
    def one(position, shards_of):
        steps = jax.random.uniform(jax.random.fold_in(jax.random.fold_in(key, 6), position), (shards_of,), jnp.float32, least / len(shards), largest / len(shards))
        return jnp.repeat(jnp.exp(steps), extent[position] // shards_of).reshape((-1,) + (1,) * (len(extent) - position - 1))

    loudness = one(*shards[0])
    for cut in shards[1:]:
        loudness = loudness * one(*cut)
    return loudness


def centred(key, extent, spread, limit, shards=(), kind=jnp.bfloat16):
    drawn = jax.random.normal(key, extent, jnp.float32) * spread
    if len(shards) > 0:
        drawn = block_scale(key, extent, shards, -0.22, 0.18) * drawn
    return jnp.clip(drawn, min=-limit, max=limit).astype(kind)


def gaussian_with(own_key, shape, scale, limit, shards, heavy, kind=jnp.bfloat16):
    result = scale * jax.random.normal(own_key, shape, jnp.float32)
    if shards:
        result = result * block_scale(own_key, shape, shards, -0.22, 0.18)
    return jnp.clip(strengthened(result, jax.random.fold_in(own_key, 3), *heavy), -limit, limit).astype(kind)


def setup_inputs(seed: int = 0) -> dict:
    seeds = jax.random.split(jax.random.key(seed), 11)
    slip = centred(seeds[0], (M, NC), 1.0, 6.0, ((1, 32),))
    lowrank_u = centred(seeds[1], (N_COL, GC, N_COL * RB * KMAX), BLK ** -0.5, 0.5, ((1, 8), (2, 4)))
    lowrank_v = gaussian_with(seeds[2], (N_COL, N_COL * RB, N_ROW * CB * KMAX, BLK), (KMAX * N_COL * N_ROW * CB) ** -0.5, 0.09375, ((1, 4), (2, 8)), (2, 1, 8, 2.0))
    ranks = plant(jax.random.randint(seeds[3], (N_COL, N_ROW * CB, N_COL * RB), KMAX // 4, KMAX + 1), jax.random.fold_in(seeds[3], 1), KMAX // 4, KMAX).astype(jnp.int32)
    near_slot = draw_near_slot(jax.random.fold_in(seeds[10], 71), 0)
    near_blocks = centred(seeds[5], (N_COL, GC, N_COL * NEAR * BLK), (BLK * N_COL * N_ROW * CB * NEAR // RB) ** -0.5, 0.09375, ((1, 8), (2, 4)))
    velocity = jnp.clip(jnp.exp(math.log(3.0) - 2.3025851 * jax.random.uniform(seeds[6], (M, NR), jnp.float32) ** block_scale(seeds[6], (M, NR), ((1, 32),), -0.2, 0.2)), 0.3, 3.0)
    theta = jnp.clip(jnp.exp(math.log(3.0) - 2.3025851 * jax.random.uniform(seeds[7], (M, NR), jnp.float32) ** block_scale(seeds[7], (M, NR), ((1, 32),), -0.2, 0.2)), 0.3, 3.0)
    a_sigma = jnp.clip(jnp.exp(math.log(2.0) - 1.3862944 * jax.random.uniform(seeds[8], (NR,), jnp.float32) ** block_scale(seeds[8], (NR,), ((0, 32),), -0.2, 0.2)), 0.5, 2.0)
    b_sigma = jnp.clip(jnp.exp(math.log(2.0) - 1.3862944 * jax.random.uniform(seeds[9], (NR,), jnp.float32) ** block_scale(seeds[9], (NR,), ((0, 32),), -0.2, 0.2)), 0.5, 2.0)
    return {"slip": slip, "lowrank_u": lowrank_u, "lowrank_v": lowrank_v, "ranks": ranks, "near_slot": near_slot, "near_blocks": near_blocks, "velocity": velocity, "theta": theta, "a_sigma": a_sigma, "b_sigma": b_sigma}


def section_stress(source_rows, left_factor, right_factor, block_ranks, slot_rows, dense_blocks):
    members, count, width = source_rows.shape
    receivers = block_ranks.shape[1]
    kmax_here = left_factor.shape[1] // receivers
    slots = slot_rows.shape[1]
    projected = jnp.einsum("mbs,bsq->mbq", source_rows.astype(jnp.float32),
                           left_factor.reshape(count, width, receivers * kmax_here).astype(jnp.float32),
                           precision=lax.Precision.HIGHEST)
    projected = projected.reshape(members, count, receivers, kmax_here)
    offsets = (jnp.arange(slots, dtype=jnp.int32) // NEAR) * RB
    targets = slot_rows + offsets[None, :]
    near_hits = targets[:, :, None] == jnp.arange(receivers, dtype=jnp.int32)[None, None, :]
    nearby = jnp.any(near_hits, axis=1)
    keep_mask = (jnp.arange(kmax_here, dtype=jnp.int32)[None, None, :] < block_ranks[:, :, None]) & (~nearby[:, :, None])
    coeffs = jnp.where(keep_mask[None], projected, 0.0).astype(jnp.bfloat16)
    far_part = jnp.einsum("mbjk,jbkr->mjr", coeffs.astype(jnp.float32),
                          right_factor.reshape(receivers, count, kmax_here, width).astype(jnp.float32),
                          precision=lax.Precision.HIGHEST)
    dense_out = jnp.einsum("mbs,bsqr->mbqr", source_rows.astype(jnp.float32),
                           dense_blocks.reshape(count, width, slots, width).astype(jnp.float32),
                           precision=lax.Precision.HIGHEST)
    near_part = jnp.einsum("mbqr,bqj->mjr", dense_out, near_hits.astype(jnp.float32),
                           precision=lax.Precision.HIGHEST)
    return (far_part + near_part).reshape(members, receivers * width)


def reference(slip, lowrank_u, lowrank_v, ranks, near_slot, near_blocks, velocity, theta, a_sigma, b_sigma):
    groups = lowrank_u.shape[0]
    group_width = lowrank_u.shape[1]
    members = slip.shape[0]
    stress_rate = jnp.zeros(velocity.shape, jnp.float32)
    for section_index in range(groups):
        source_rows = slip[:, section_index * group_width:(section_index + 1) * group_width]
        source_rows = source_rows.reshape(members, group_width // BLK, BLK)
        stress_rate = stress_rate + section_stress(source_rows, lowrank_u[section_index], lowrank_v[section_index],
                                                 ranks[section_index], near_slot[section_index], near_blocks[section_index])
    theta_rate = 1.0 - velocity * theta
    accel = (stress_rate - b_sigma[None, :] * theta_rate / theta) / (a_sigma[None, :] / velocity + 0.5)
    return stress_rate, accel
```

```python
import functools

import jax
import jax.numpy as jnp
from jax import lax
from jax.experimental import pallas as pl
from jax.experimental.pallas import tpu as pltpu
from jax.sharding import PartitionSpec as P

BF16, F32, I32 = jnp.bfloat16, jnp.float32, jnp.int32
LANES = 128
VMEM_LIMIT = 16 * 2**20


def dot(left, right):
    return jnp.dot(left, right, preferred_element_type=F32)


def keep_masks(ranks, slots):
    count, receivers = ranks.shape
    kmax = 32
    width = receivers * kmax
    block = lax.broadcasted_iota(I32, (count, receivers), 1)
    for slot in range(slots.shape[1]):
        ranks = jnp.where(slots[:, slot : slot + 1] == block, 0, ranks)
    lane = lax.broadcasted_iota(I32, (receivers, width), 1)
    spread = lane // kmax == lax.broadcasted_iota(I32, (receivers, width), 0)
    wide = dot(ranks.astype(F32).astype(BF16), spread.astype(BF16))
    rank_index = lax.broadcasted_iota(I32, (count, width), 1) % kmax
    return (rank_index.astype(F32) < wide).astype(F32)


def regrouped(parts, lane):
    half = lane >= 64
    odd = (lane // 32) % 2 == 1
    swapped = [None] * 4
    for i in range(2):
        low, high = parts[i], parts[i + 2]
        swapped[i] = jnp.where(half, pltpu.roll(high, 64, 1), low)
        swapped[i + 2] = jnp.where(half, high, pltpu.roll(low, 64, 1))
    out = [None] * 4
    for i in (0, 2):
        low, high = swapped[i], swapped[i + 1]
        out[i] = jnp.where(odd, pltpu.roll(high, 32, 1), low)
        out[i + 1] = jnp.where(odd, high, pltpu.roll(low, 96, 1))
    return out


def add_section(slip, u_ref, v_ref, near_ref, ranks, slots, slot_at, total, coeffs):
    receivers = total.shape[0]
    count = ranks.shape[0]
    kept = keep_masks(ranks, slots)
    lane = lax.broadcasted_iota(I32, (1, LANES), 1)
    for first in range(0, count, 4):
        projected = []
        for b in range(first, first + 4):
            rows = slice(b * LANES, (b + 1) * LANES)
            value = dot(slip[:, rows], u_ref[rows, :])
            projected.append(jnp.where(kept[b : b + 1, :] > 0, value, 0.0))
        for group in range(receivers // 4):
            lanes = slice(group * LANES, (group + 1) * LANES)
            pieces = regrouped([p[:, lanes] for p in projected], lane)
            for i, piece in enumerate(pieces):
                coeffs[group * 4 + i, :, first * 32 : (first + 4) * 32] = piece.astype(BF16)
    for b in range(count):
        rows = slice(b * LANES, (b + 1) * LANES)
        dense = dot(slip[:, rows], near_ref[rows, :])
        for slot in range(slots.shape[1]):
            total[slot_at(b, slot)] += dense[:, slot * LANES : (slot + 1) * LANES]
    for j in range(receivers):
        total[j] += dot(coeffs[j], v_ref[j])


def stress_kernel(axis, offsets, final, *refs):
    slips = refs[: len(offsets)]
    u_ref, v_ref, near_ref, ranks_ref, slots_ref, slots_smem = refs[len(offsets) : len(offsets) + 6]
    rest = refs[len(offsets) + 6 :]
    if len(rest) == 4:
        start_ref, out_ref, total, coeffs = rest
        total[...] = start_ref[...]
    else:
        out_ref, total, coeffs = rest
        total[...] = jnp.zeros_like(total)
    me = lax.axis_index(axis)
    for slip_ref, offset in zip(slips, offsets):
        s = me ^ offset
        add_section(
            slip_ref[...],
            u_ref.at[s],
            v_ref.at[s],
            near_ref.at[s],
            ranks_ref[s],
            slots_ref[s],
            lambda b, slot: slots_smem[s, b, slot],
            total,
            coeffs,
        )
    if not final:
        out_ref[...] = total[...]
    else:
        owners, _, owned = out_ref.shape
        for r in range(owners):
            for at in range(0, owned, LANES):
                take = min(owned, LANES)
                j, lane = divmod(r * owned + at, LANES)
                out_ref[r, :, at : at + take] = total[j, :, lane : lane + take].astype(BF16)


def stress(slips, offsets, weights, start, out_shape, final):
    u, v, near, ranks, slots = weights
    members = slips[0].shape[0]
    receivers, kdim = v.shape[1], v.shape[2]
    used = len(slips) * (u.size + v.size + near.size) // u.shape[0]
    vmem = pl.BlockSpec(memory_space=pltpu.VMEM)
    args = [*slips, u, v, near, ranks, slots, slots]
    specs = [vmem] * (len(args) - 1) + [pl.BlockSpec(memory_space=pltpu.SMEM)]
    if start is not None:
        args.append(start)
        specs.append(vmem)
    return pl.pallas_call(
        functools.partial(stress_kernel, "col", offsets, final),
        out_shape=out_shape,
        in_specs=specs,
        out_specs=vmem,
        scratch_shapes=[
            pltpu.VMEM((receivers, members, LANES), F32),
            pltpu.VMEM((receivers, members, kdim), BF16),
        ],
        compiler_params=pltpu.CompilerParams(vmem_limit_bytes=VMEM_LIMIT),
        cost_estimate=pl.CostEstimate(
            flops=2 * members * used,
            bytes_accessed=2 * used,
            transcendentals=0,
        ),
    )(*args)


def swapped_with(value, offset, groups):
    return lax.ppermute(value, "col", [(i, i ^ offset) for i in range(groups)])


def body(
    slip, lowrank_u, lowrank_v, ranks, near_slot, near_blocks, velocity, theta, a_sigma, b_sigma
):
    groups = lax.axis_size("col")
    owners = lax.axis_size("row")
    members = slip.shape[0]
    receivers = lowrank_v.shape[1]
    owned = velocity.shape[1]
    weights = [
        pltpu.with_memory_space_constraint(w, pltpu.VMEM) for w in (lowrank_u, lowrank_v, near_blocks)
    ] + [ranks, near_slot]
    across = swapped_with(slip, 2, groups)
    sibling = swapped_with(slip, 1, groups)
    total_shape = jax.ShapeDtypeStruct((receivers, members, LANES), F32)
    total = stress([slip, sibling], (0, 1), weights, None, total_shape, False)
    beyond = swapped_with(across, 1, groups)
    total = stress([across], (2,), weights, total, total_shape, False)
    sent_shape = jax.ShapeDtypeStruct((owners, members, owned), BF16)
    sent = stress([beyond], (3,), weights, total, sent_shape, True)
    received = lax.all_to_all(sent, "row", 0, 0, tiled=True)
    owned_rows = jnp.sum(received.astype(F32), axis=0)
    theta_rate = 1.0 - velocity * theta
    accel = (owned_rows - b_sigma[None, :] * theta_rate / theta) / (
        a_sigma[None, :] / velocity + 0.5
    )
    return (owned_rows, accel)


def solution(mesh):
    placed = (
        P(None, ("col", "row")),
        P(None, "row", "col"),
        P(None, "col", "row", None),
        P(None, "row", "col"),
        P(None, "row", "col"),
        P(None, "row", "col"),
        P(None, ("col", "row")),
        P(None, ("col", "row")),
        P(("col", "row")),
        P(("col", "row")),
    )
    return jax.shard_map(
        body,
        mesh=mesh,
        in_specs=placed,
        out_specs=(P(None, ("col", "row")), P(None, ("col", "row"))),
        check_vma=False,
    )
```

```python
import functools

import jax
import jax.numpy as jnp
from jax import lax
from jax.experimental import pallas as pl
from jax.experimental.pallas import tpu as pltpu
from jax.sharding import PartitionSpec as P

BF16, F32, I32 = jnp.bfloat16, jnp.float32, jnp.int32
LANES = 128
KMAX = 32
VMEM_LIMIT = 32 * 2**20
HBM_SPEC = pl.BlockSpec(memory_space=pltpu.HBM)
VMEM_SPEC = pl.BlockSpec(memory_space=pltpu.VMEM)


def dot(left, right):
    return jnp.dot(left, right, preferred_element_type=F32)


def regrouped(parts, lane):
    half = lane >= 64
    odd = (lane // KMAX) % 2 == 1
    swapped = [None] * 4
    for i in range(2):
        low, high = parts[i], parts[i + 2]
        swapped[i] = jnp.where(half, pltpu.roll(high, 64, 1), low)
        swapped[i + 2] = jnp.where(half, high, pltpu.roll(low, 64, 1))
    out = [None] * 4
    for i in (0, 2):
        low, high = swapped[i], swapped[i + 1]
        out[i] = jnp.where(odd, pltpu.roll(high, 32, 1), low)
        out[i + 1] = jnp.where(odd, high, pltpu.roll(low, 96, 1))
    return out


def add_section(slip, u_ref, v_ref, near_ref, kept_ref, slot_at, start, total, coeffs):
    receivers = total.shape[0]
    count = kept_ref.shape[0]
    slots = near_ref.shape[1] // LANES
    lane = lax.broadcasted_iota(I32, (1, LANES), 1)
    for first in range(0, count, 4):
        projected = []
        for b in range(first, first + 4):
            rows = slice(b * LANES, (b + 1) * LANES)
            value = dot(slip[:, rows], u_ref[rows, :])
            projected.append(jnp.where(kept_ref[b : b + 1, :] > 0, value, 0.0))
        for group in range(receivers // 4):
            lanes = slice(group * LANES, (group + 1) * LANES)
            pieces = regrouped([p[:, lanes] for p in projected], lane)
            for i, piece in enumerate(pieces):
                coeffs[group * 4 + i, :, first * KMAX : (first + 4) * KMAX] = piece.astype(BF16)
    for j in range(receivers):
        value = dot(coeffs[j], v_ref[j])
        total[j] = value if start is None else start[j] + value
    for b in range(count):
        rows = slice(b * LANES, (b + 1) * LANES)
        dense = dot(slip[:, rows], near_ref[rows, :])
        for slot in range(slots):
            total[slot_at(slot, b)] += dense[:, slot * LANES : (slot + 1) * LANES]


def first_kernel(
    slip_hbm, sibling, u_hbm, v_hbm, near_hbm, ranks_hbm, slots_hbm, velocity_hbm, theta_hbm,
    a_hbm, b_hbm,
    total, u_out, v_out, near_out, kept_out, gain, shift,
    slip, u_in, v_in, near_in, ranks, slots, velocity, theta, a_sigma, b_sigma, kept, coeffs, sems,
):
    me = lax.axis_index("col")
    used = iter(range(sems.shape[0]))

    def fetch(source, target):
        copy = pltpu.make_async_copy(source, target, sems.at[next(used)])
        copy.start()
        return copy

    small = [fetch(ranks_hbm, ranks), fetch(slots_hbm, slots)]
    loads = []
    for i in range(2):
        s = me ^ i
        loads.append([fetch(u_hbm.at[s], u_in.at[i])])
        if i == 0:
            loads[0].append(fetch(slip_hbm, slip))
        loads[i].append(fetch(v_hbm.at[s], v_in.at[i]))
        loads[i].append(fetch(near_hbm.at[s], near_in.at[i]))
    params = [
        fetch(velocity_hbm, velocity),
        fetch(theta_hbm, theta),
        fetch(a_hbm, a_sigma),
        fetch(b_hbm, b_sigma),
    ]
    later = []
    for i in range(2):
        s = me ^ (2 + i)
        later.append(fetch(u_hbm.at[s], u_out.at[i]))
        later.append(fetch(v_hbm.at[s], v_out.at[i]))
        later.append(fetch(near_hbm.at[s], near_out.at[i]))

    for copy in small:
        copy.wait()
    _, count, receivers = ranks.shape
    width = receivers * KMAX
    column = lax.broadcasted_iota(I32, (receivers, width), 1)
    spread = column // KMAX == lax.broadcasted_iota(I32, (receivers, width), 0)
    lane = lax.broadcasted_iota(I32, (1, width), 1)
    block, index = lane // KMAX, (lane % KMAX).astype(F32)
    for i in range(4):
        s = me ^ i
        wide = dot(ranks[s].astype(F32).astype(BF16), spread.astype(BF16))
        target = kept.at[i] if i < 2 else kept_out.at[i - 2]
        for b in range(count):
            keep = index < wide[b : b + 1, :]
            for slot in range(slots.shape[1]):
                keep = keep & (block != slots[s, slot, b])
            target[b : b + 1, :] = keep.astype(F32)

    for i in range(2):
        s = me ^ i
        for copy in loads[i]:
            copy.wait()
        add_section(
            slip[...] if i == 0 else sibling[...],
            u_in.at[i], v_in.at[i], near_in.at[i], kept.at[i],
            lambda slot, b: slots[s, slot, b],
            None if i == 0 else total, total, coeffs,
        )
    for copy in params:
        copy.wait()
    rate, state = velocity[...], theta[...]
    divisor = 1.0 / (a_sigma[...] / rate + 0.5)
    gain[...] = divisor
    shift[...] = -(b_sigma[...] * (1.0 - rate * state) / state) * divisor
    for copy in later:
        copy.wait()


def later_kernel(which, final, slip, u_ref, v_ref, near_ref, kept, slots_hbm, start, *refs):
    me = lax.axis_index("col")
    s = me ^ (2 + which)
    if final:
        sent, own, total, slots, coeffs, sem = refs
    else:
        total, slots, coeffs, sem = refs
    copy = pltpu.make_async_copy(slots_hbm, slots, sem)
    copy.start()
    waited = []

    def slot_at(slot, b):
        if not waited:
            copy.wait()
            waited.append(True)
        return slots[s, slot, b]

    add_section(
        slip[...], u_ref.at[which], v_ref.at[which], near_ref.at[which], kept.at[which],
        slot_at, start, total, coeffs,
    )
    if not final:
        return
    owners, _, owned = sent.shape
    row = lax.axis_index("row")
    for r in range(owners):
        for at in range(0, owned, LANES):
            take = min(owned, LANES)
            j, lane = divmod(r * owned + at, LANES)
            sent[r, :, at : at + take] = total[j, :, lane : lane + take].astype(BF16)
    sent[row] = jnp.zeros(own.shape, BF16)
    if owned % LANES == 0:
        blocks = owned // LANES
        for i in range(blocks):
            own[:, i * LANES : (i + 1) * LANES] = total[row * blocks + i]
    else:
        value = jnp.zeros(own.shape, F32)
        for r in range(owners):
            j, lane = divmod(r * owned, LANES)
            value = jnp.where(row == r, total[j, :, lane : lane + owned], value)
        own[...] = value


def in_hbm(value):
    return pltpu.with_memory_space_constraint(value, pltpu.HBM)


def params(flops, size):
    return dict(
        compiler_params=pltpu.CompilerParams(vmem_limit_bytes=VMEM_LIMIT),
        cost_estimate=pl.CostEstimate(flops=flops, bytes_accessed=size, transcendentals=0),
    )


def body(
    slip, lowrank_u, lowrank_v, ranks, near_slot, near_blocks, velocity, theta, a_sigma, b_sigma
):
    groups, owners = lax.axis_size("col"), lax.axis_size("row")
    members = slip.shape[0]
    _, receivers, depth, _ = lowrank_v.shape
    owned = velocity.shape[1]
    _, count, slots = near_slot.shape
    weights = (lowrank_u, lowrank_v, near_blocks)
    size = sum(w.size for w in weights) // groups
    slots_by = jnp.swapaxes(near_slot, 1, 2)

    def swapped_with(value, offset):
        return lax.ppermute(value, "col", [(i, i ^ offset) for i in range(groups)])

    across = swapped_with(slip, 2)
    sibling = swapped_with(slip, 1)

    def two(w):
        return (2,) + w.shape[1:]

    kept_shape = (2, count, receivers * KMAX)
    coeffs = pltpu.VMEM((receivers, members, depth), BF16)
    total_shape = pltpu.VMEM((receivers, members, LANES), F32)
    row_shape = velocity.shape
    total, u_two, v_two, near_two, kept, gain, shift = pl.pallas_call(
        first_kernel,
        out_shape=(
            [total_shape]
            + [pltpu.VMEM(two(w), BF16) for w in weights]
            + [pltpu.VMEM(kept_shape, F32), pltpu.VMEM(row_shape, F32), pltpu.VMEM(row_shape, F32)]
        ),
        in_specs=[HBM_SPEC, VMEM_SPEC] + [HBM_SPEC] * 9,
        out_specs=[VMEM_SPEC] * 7,
        scratch_shapes=[
            pltpu.VMEM(slip.shape, BF16),
            *[pltpu.VMEM(two(w), BF16) for w in weights],
            pltpu.VMEM(ranks.shape, I32),
            pltpu.SMEM(slots_by.shape, I32),
            pltpu.VMEM(row_shape, F32),
            pltpu.VMEM(row_shape, F32),
            pltpu.VMEM((1, owned), F32),
            pltpu.VMEM((1, owned), F32),
            pltpu.VMEM(kept_shape, F32),
            coeffs,
            pltpu.SemaphoreType.DMA((19,)),
        ],
        **params(4 * members * size, 8 * size),
    )(
        in_hbm(slip), sibling, *map(in_hbm, weights), in_hbm(ranks), in_hbm(slots_by),
        in_hbm(velocity), in_hbm(theta),
        in_hbm(a_sigma.reshape(1, owned)), in_hbm(b_sigma.reshape(1, owned)),
    )
    across, total = lax.optimization_barrier((across, total))

    def later(which, value, total):
        final = which == 1
        if final:
            out_shape = [
                jax.ShapeDtypeStruct((owners, members, owned), BF16),
                pltpu.VMEM((members, owned), F32),
            ]
        else:
            out_shape = [total_shape]
        return pl.pallas_call(
            functools.partial(later_kernel, which, final),
            out_shape=out_shape,
            in_specs=[VMEM_SPEC] * 5 + [HBM_SPEC, VMEM_SPEC],
            out_specs=[VMEM_SPEC] * len(out_shape),
            scratch_shapes=([total_shape] if final else [])
            + [pltpu.SMEM(slots_by.shape, I32), coeffs, pltpu.SemaphoreType.DMA],
            **params(2 * members * size, 2 * size),
        )(value, u_two, v_two, near_two, kept, in_hbm(slots_by), total)

    beyond = swapped_with(across, 1)
    (total,) = later(0, across, total)
    sent, own = later(1, beyond, total)
    received = lax.all_to_all(sent, "row", 0, 0, tiled=True)
    stress_rate = own + jnp.sum(received.astype(F32), axis=0)
    return (stress_rate, stress_rate * gain + shift)


def solution(mesh):
    placed = (
        P(None, ("col", "row")),
        P(None, "row", "col"),
        P(None, "col", "row", None),
        P(None, "row", "col"),
        P(None, "row", "col"),
        P(None, "row", "col"),
        P(None, ("col", "row")),
        P(None, ("col", "row")),
        P(("col", "row")),
        P(("col", "row")),
    )
    return jax.shard_map(
        body,
        mesh=mesh,
        in_specs=placed,
        out_specs=(P(None, ("col", "row")), P(None, ("col", "row"))),
        check_vma=False,
    )
```

```python
import functools

import jax
import jax.numpy as jnp
from jax import lax
from jax.experimental import pallas as pl
from jax.experimental.pallas import tpu as pltpu
from jax.sharding import PartitionSpec as P

BF16, F32, I32 = jnp.bfloat16, jnp.float32, jnp.int32
LANES = 128
KMAX = 32
PACK = LANES // KMAX
VMEM_LIMIT = 32 * 2**20
HBM_SPEC = pl.BlockSpec(memory_space=pltpu.HBM)
VMEM_SPEC = pl.BlockSpec(memory_space=pltpu.VMEM)
SMEM_SPEC = pl.BlockSpec(memory_space=pltpu.SMEM)


def dot(left, right):
    return jnp.dot(left, right, preferred_element_type=F32)


def add_far(slip, u_ref, v_ref, kept_ref, total, coeffs, fresh=False):
    count, width = kept_ref.shape
    place = lax.broadcasted_iota(I32, (1, LANES), 1) // KMAX
    for first in range(0, count, PACK):
        projected = []
        for b in range(first, first + PACK):
            rows = slice(b * LANES, (b + 1) * LANES)
            value = dot(slip[:, rows], u_ref[rows, :])
            projected.append(jnp.where(kept_ref[b : b + 1, :] > 0, value, 0.0))
        for g in range(width // LANES):
            turned = []
            for i, value in enumerate(projected):
                value = value[:, g * LANES : (g + 1) * LANES]
                value = pltpu.roll(value, i * KMAX, 1) if i else value
                turned.append(value.astype(BF16))
            for i in range(PACK):
                row = turned[-i % PACK]
                for c in range(1, PACK):
                    row = jnp.where(place == c, turned[(c - i) % PACK], row)
                coeffs[g * PACK + i, :, first * KMAX : (first + PACK) * KMAX] = row
    for j in range(total.shape[0]):
        order = []
        for first in range(0, count, PACK):
            order += [first + (c - j) % PACK for c in range(PACK)]
        right = jnp.concatenate([v_ref[j, b * KMAX : (b + 1) * KMAX, :] for b in order], axis=0)
        value = dot(coeffs[j], right)
        total[j] = value if fresh else total[j] + value


def add_near(slip, near_ref, slots, s, total):
    count = near_ref.shape[0] // LANES
    for b in range(count):
        rows = slice(b * LANES, (b + 1) * LANES)
        dense = dot(slip[:, rows], near_ref[rows, :])
        for slot in range(near_ref.shape[1] // LANES):
            total[slots[s, slot, b]] += dense[:, slot * LANES : (slot + 1) * LANES]


class Fetches:
    def __init__(self, sems):
        self.sems, self.used = sems, 0

    def __call__(self, source, target):
        copy = pltpu.make_async_copy(source, target, self.sems.at[self.used])
        self.used += 1
        copy.start()
        return copy


def wait_all(copies):
    for copy in copies:
        copy.wait()


def own_kernel(
    slip_hbm, u_hbm, v_hbm, near_hbm, ranks_hbm, slots_hbm, velocity_hbm, theta_hbm, a_hbm, b_hbm,
    total, u_out, v_out, near_out, kept, gain, shift, slots,
    slip, u_in, v_in, near_in, ranks, velocity, theta, a_sigma, b_sigma, coeffs, sems,
):
    me = lax.axis_index("col")
    fetch = Fetches(sems)
    small = [fetch(ranks_hbm, ranks), fetch(slots_hbm, slots)]
    mine = [
        fetch(slip_hbm, slip),
        fetch(u_hbm.at[me], u_in),
        fetch(v_hbm.at[me], v_in),
        fetch(near_hbm.at[me], near_in),
    ]
    later = []
    for i in range(3):
        s = me ^ (1 + i)
        later += [
            fetch(u_hbm.at[s], u_out.at[i]),
            fetch(v_hbm.at[s], v_out.at[i]),
            fetch(near_hbm.at[s], near_out.at[i]),
        ]
    fields = [
        fetch(velocity_hbm, velocity),
        fetch(theta_hbm, theta),
        fetch(a_hbm, a_sigma),
        fetch(b_hbm, b_sigma),
    ]
    wait_all(small)
    _, count, receivers = ranks.shape
    width = receivers * KMAX
    column = lax.broadcasted_iota(I32, (receivers, width), 1)
    spread = column // KMAX == lax.broadcasted_iota(I32, (receivers, width), 0)
    lane = lax.broadcasted_iota(I32, (1, width), 1)
    block, index = lane // KMAX, (lane % KMAX).astype(F32)
    for i in range(4):
        s = me ^ i
        wide = dot(ranks[s].astype(F32).astype(BF16), spread.astype(BF16))
        for b in range(count):
            keep = index < wide[b : b + 1, :]
            for slot in range(slots.shape[1]):
                keep = keep & (block != slots[s, slot, b])
            kept[i, b : b + 1, :] = keep.astype(F32)

    wait_all(mine)
    add_far(slip[...], u_in, v_in, kept.at[0], total, coeffs, fresh=True)
    add_near(slip[...], near_in, slots, me, total)
    wait_all(later)
    wait_all(fields)
    rate, state = velocity[...], theta[...]
    divisor = 1.0 / (a_sigma[...] / rate + 0.5)
    gain[...] = divisor
    shift[...] = -(b_sigma[...] * (1.0 - rate * state) / state) * divisor


def later_kernel(offsets, final, *refs):
    slips, refs = refs[: len(offsets)], refs[len(offsets) :]
    u_ref, v_ref, near_ref, kept, slots, start, total, *refs = refs
    *sent, coeffs = refs
    me = lax.axis_index("col")
    for slip, i in zip(slips, offsets):
        add_far(slip[...], u_ref.at[i - 1], v_ref.at[i - 1], kept.at[i], total, coeffs)
        add_near(slip[...], near_ref.at[i - 1], slots, me ^ i, total)
    if not final:
        return
    owners = lax.axis_size("row")
    blocks = total.shape[0] // PACK
    mine = lax.axis_index("row") // (owners // blocks)
    for k, target in enumerate(sent):
        for i in range(PACK):
            target[i] = total[(mine ^ k) * PACK + i].astype(target.dtype)


def gather_kernel(place, *refs):
    own, *received, sent, kept, total = refs
    for i in range(PACK):
        value = own[i]
        for part in received:
            value = value + part[i].astype(F32)
        total[i] = value
    side = (lax.axis_index("row") >> place) & 1
    low, owned = 1 << place, sent.shape[2]
    for n in range(sent.shape[0]):
        high, low_n = divmod(n, low)
        for at in range(0, owned, LANES):
            take = min(owned, LANES)
            block, lane = divmod(low_n * owned + at, LANES)
            for target, half in ((sent, 1 - side), (kept, side)):
                base = (2 * high + half) * (low * owned // LANES)
                target[n, :, at : at + take] = total[base + block][:, lane : lane + take]


def halve_kernel(place, kept, received, sent, own):
    side = (lax.axis_index("row") >> place) & 1
    low = 1 << place
    for n in range(sent.shape[0]):
        base = (n // low) * 2 * low + n % low
        for target, half in ((sent, 1 - side), (own, side)):
            i = base + half * low
            target[n] = kept[i] + received[i]


def in_hbm(value):
    return pltpu.with_memory_space_constraint(value, pltpu.HBM)


def params(flops, size):
    return dict(
        compiler_params=pltpu.CompilerParams(vmem_limit_bytes=VMEM_LIMIT),
        cost_estimate=pl.CostEstimate(flops=flops, bytes_accessed=size, transcendentals=0),
    )


def body(
    slip, lowrank_u, lowrank_v, ranks, near_slot, near_blocks, velocity, theta, a_sigma, b_sigma
):
    groups, owners = lax.axis_size("col"), lax.axis_size("row")
    members = slip.shape[0]
    _, receivers, depth, _ = lowrank_v.shape
    owned = velocity.shape[1]
    _, count, _ = near_slot.shape
    n_groups = receivers // PACK
    per_group = owners // n_groups
    slots_by = jnp.swapaxes(near_slot, 1, 2)
    size = (lowrank_u.size + lowrank_v.size + near_blocks.size) // groups

    def col_swap(value, offset):
        return lax.ppermute(value, "col", [(i, i ^ offset) for i in range(groups)])

    def row_swap(value, offset):
        return lax.ppermute(value, "row", [(i, i ^ offset) for i in range(owners)])

    across = col_swap(slip, 2)
    sibling = col_swap(slip, 1)

    weights = (lowrank_u, lowrank_v, near_blocks)
    field = pltpu.VMEM(velocity.shape, F32)
    coeffs = pltpu.VMEM((receivers, members, depth), BF16)
    total_shape = pltpu.VMEM((receivers, members, LANES), F32)
    slots_smem = pltpu.SMEM(slots_by.shape, I32)
    total, u_later, v_later, near_later, kept, gain, shift, slots = pl.pallas_call(
        own_kernel,
        out_shape=[
            total_shape,
            *[pltpu.VMEM((3, *w.shape[1:]), BF16) for w in weights],
            pltpu.VMEM((groups, count, receivers * KMAX), F32), field, field, slots_smem,
        ],
        in_specs=[HBM_SPEC] * 10,
        out_specs=[VMEM_SPEC] * 7 + [SMEM_SPEC],
        scratch_shapes=[
            pltpu.VMEM(slip.shape, BF16),
            *[pltpu.VMEM(w.shape[1:], BF16) for w in weights],
            pltpu.VMEM(ranks.shape, I32), field, field,
            pltpu.VMEM((1, owned), F32), pltpu.VMEM((1, owned), F32),
            coeffs, pltpu.SemaphoreType.DMA((19,)),
        ],
        **params(2 * members * size, 8 * size),
    )(
        *map(
            in_hbm,
            (
                slip, *weights, ranks, slots_by, velocity, theta,
                a_sigma.reshape(1, owned), b_sigma.reshape(1, owned),
            ),
        )
    )
    across, total = lax.optimization_barrier((across, total))

    def later(offsets, slips, total):
        final = offsets[-1] == 3
        out_shape = [total_shape]
        if final:
            shape = (PACK, members, LANES)
            out_shape += [pltpu.VMEM(shape, BF16 if k else F32) for k in range(n_groups)]
        return pl.pallas_call(
            functools.partial(later_kernel, offsets, final),
            out_shape=out_shape,
            in_specs=[VMEM_SPEC] * (len(slips) + 4) + [SMEM_SPEC, VMEM_SPEC],
            out_specs=[VMEM_SPEC] * len(out_shape),
            scratch_shapes=[coeffs],
            input_output_aliases={len(slips) + 5: 0},
            **params(2 * members * size * len(slips), 2 * size * len(slips)),
        )(*slips, u_later, v_later, near_later, kept, slots, total)

    beyond = col_swap(across, 1)
    (total,) = later((1, 2), (sibling, across), total)
    _, own, *sent = later((3,), (beyond,), total)
    order = (1, 2, 0)
    received = [row_swap(sent[k], (k + 1) * per_group) for k in order]
    place = per_group.bit_length() - 2
    shape = (per_group // 2, members, owned)
    sent, own = pl.pallas_call(
        functools.partial(gather_kernel, place),
        out_shape=[pltpu.VMEM(shape, F32)] * 2,
        in_specs=[VMEM_SPEC] * (1 + len(received)),
        out_specs=[VMEM_SPEC] * 2,
        scratch_shapes=[pltpu.VMEM((PACK, members, LANES), F32)],
        **params(0, 40 * own.size),
    )(own, *received)
    received = row_swap(sent, 1 << place)
    for place in reversed(range(place)):
        shape = (own.shape[0] // 2, members, owned)
        sent, own = pl.pallas_call(
            functools.partial(halve_kernel, place),
            out_shape=[pltpu.VMEM(shape, F32)] * 2,
            in_specs=[VMEM_SPEC] * 2,
            out_specs=[VMEM_SPEC] * 2,
            **params(0, 12 * own.size),
        )(own, received)
        received = row_swap(sent, 1 << place)
    stress_rate = own[0] + received[0]
    return (stress_rate, stress_rate * gain + shift)


def solution(mesh):
    placed = (
        P(None, ("col", "row")),
        P(None, "row", "col"),
        P(None, "col", "row", None),
        P(None, "row", "col"),
        P(None, "row", "col"),
        P(None, "row", "col"),
        P(None, ("col", "row")),
        P(None, ("col", "row")),
        P(("col", "row")),
        P(("col", "row")),
    )
    return jax.shard_map(
        body,
        mesh=mesh,
        in_specs=placed,
        out_specs=(P(None, ("col", "row")), P(None, ("col", "row"))),
        check_vma=False,
    )
```

```python
import functools

import jax
import jax.numpy as jnp
from jax import lax
from jax.experimental import pallas as pl
from jax.experimental.pallas import tpu as pltpu
from jax.sharding import PartitionSpec as P

BF16, F32, I32 = jnp.bfloat16, jnp.float32, jnp.int32
LANES = 128
KMAX = 32
PACK = LANES // KMAX
VMEM_LIMIT = 32 * 2**20
PAD = 16
HBM_SPEC = pl.BlockSpec(memory_space=pltpu.HBM)
VMEM_SPEC = pl.BlockSpec(memory_space=pltpu.VMEM)
SMEM_SPEC = pl.BlockSpec(memory_space=pltpu.SMEM)


def dot(left, right):
    return jnp.dot(left, right, preferred_element_type=F32)


def add_far(slip, u_ref, v_ref, kept_ref, total, coeffs, fresh=False):
    count, width = kept_ref.shape
    place = lax.broadcasted_iota(I32, (1, LANES), 1) // KMAX
    for first in range(0, count, PACK):
        projected = []
        for b in range(first, first + PACK):
            rows = slice(b * LANES, (b + 1) * LANES)
            value = dot(slip[:, rows], u_ref[rows, :])
            projected.append(jnp.where(kept_ref[b : b + 1, :] > 0, value, 0.0))
        for g in range(width // LANES):
            turned = []
            for i, value in enumerate(projected):
                value = value[:, g * LANES : (g + 1) * LANES]
                value = pltpu.roll(value, i * KMAX, 1) if i else value
                turned.append(value.astype(BF16))
            for i in range(PACK):
                row = turned[-i % PACK]
                for c in range(1, PACK):
                    row = jnp.where(place == c, turned[(c - i) % PACK], row)
                coeffs[g * PACK + i, :, first * KMAX : (first + PACK) * KMAX] = row
    for j in range(total.shape[0]):
        order = []
        for first in range(0, count, PACK):
            order += [first + (c - j) % PACK for c in range(PACK)]
        right = jnp.concatenate([v_ref[j, b * KMAX : (b + 1) * KMAX, :] for b in order], axis=0)
        value = dot(coeffs[j], right)
        total[j] = value if fresh else total[j] + value


def add_near(slip, near_ref, slots, s, total):
    count = near_ref.shape[0] // LANES
    for b in range(count):
        rows = slice(b * LANES, (b + 1) * LANES)
        dense = dot(slip[:, rows], near_ref[rows, :])
        for slot in range(near_ref.shape[1] // LANES):
            total[slots[s, slot, b]] += dense[:, slot * LANES : (slot + 1) * LANES]


class Fetches:
    def __init__(self, sems):
        self.sems, self.used = sems, 0

    def __call__(self, source, target):
        copy = pltpu.make_async_copy(source, target, self.sems.at[self.used])
        self.used += 1
        copy.start()
        return copy


def wait_all(copies):
    for copy in copies:
        copy.wait()


def own_kernel(
    slip_hbm, u_hbm, v_hbm, near_hbm, ranks_hbm, slots_hbm, velocity_hbm, theta_hbm, a_hbm, b_hbm,
    total, u_out, v_out, near_out, kept, gain, shift, slots,
    slip, u_in, v_in, near_in, ranks, velocity, theta, a_sigma, b_sigma, coeffs, sems,
):
    me = lax.axis_index("col")
    fetch = Fetches(sems)
    small = [fetch(ranks_hbm, ranks), fetch(slots_hbm, slots)]
    mine = [
        fetch(slip_hbm, slip),
        fetch(u_hbm.at[me], u_in),
        fetch(v_hbm.at[me], v_in),
        fetch(near_hbm.at[me], near_in),
    ]
    fields = [
        fetch(velocity_hbm, velocity),
        fetch(theta_hbm, theta),
        fetch(a_hbm, a_sigma),
        fetch(b_hbm, b_sigma),
    ]
    later = []
    for i in range(3):
        s = me ^ (1 + i)
        later += [
            fetch(u_hbm.at[s], u_out.at[i]),
            fetch(v_hbm.at[s], v_out.at[i]),
            fetch(near_hbm.at[s], near_out.at[i]),
        ]
    wait_all(small)
    _, count, receivers = ranks.shape
    width = receivers * KMAX
    column = lax.broadcasted_iota(I32, (receivers, width), 1)
    spread = column // KMAX == lax.broadcasted_iota(I32, (receivers, width), 0)
    lane = lax.broadcasted_iota(I32, (1, width), 1)
    block, index = lane // KMAX, (lane % KMAX).astype(F32)
    for i in range(4):
        s = me ^ i
        wide = dot(ranks[s].astype(F32).astype(BF16), spread.astype(BF16))
        for b in range(count):
            keep = index < wide[b : b + 1, :]
            for slot in range(slots.shape[1]):
                keep = keep & (block != slots[s, slot, b])
            kept[i, b : b + 1, :] = keep.astype(F32)

    wait_all(mine)
    add_far(slip[...], u_in, v_in, kept.at[0], total, coeffs, fresh=True)
    add_near(slip[...], near_in, slots, me, total)
    wait_all(fields)
    rate, state = velocity[...], theta[...]
    divisor = 1.0 / (a_sigma[...] / rate + 0.5)
    gain[...] = divisor
    shift[...] = -(b_sigma[...] * (1.0 - rate * state) / state) * divisor
    wait_all(later)


def later_kernel(offsets, final, *refs):
    slips, refs = refs[: len(offsets)], refs[len(offsets) :]
    u_ref, v_ref, near_ref, kept, slots, start, total, *refs = refs
    *sent, coeffs = refs
    me = lax.axis_index("col")
    for slip, i in zip(slips, offsets):
        add_far(slip[...], u_ref.at[i - 1], v_ref.at[i - 1], kept.at[i], total, coeffs)
        add_near(slip[...], near_ref.at[i - 1], slots, me ^ i, total)
    if not final:
        return
    swapped, same, other = sent
    mine, side, half = row_place(total)
    for k in range(3):
        for i in range(half):
            block = total[(mine ^ k) * PACK + (1 - side) * half + i]
            swapped[k * half + i] = block.astype(swapped.dtype)
    for target, to_side in ((same, side), (other, 1 - side)):
        target[:, total.shape[1] :, :] = jnp.zeros_like(target[:, total.shape[1] :, :])
        for i in range(half):
            write_block(target, i, total[(mine ^ 3) * PACK + to_side * half + i])


def row_place(total):
    row, groups = lax.axis_index("row"), total.shape[0] // PACK
    per_group = lax.axis_size("row") // groups
    return row // per_group, row % per_group // (per_group // 2), PACK // 2


def write_block(target, i, block):
    owned, block = target.shape[2], block.astype(target.dtype)
    if owned >= LANES:
        n, at = divmod(i * LANES, owned)
        target[n, : block.shape[0], at : at + LANES] = block
    else:
        for at in range(0, LANES, owned):
            target[(i * LANES + at) // owned, : block.shape[0], :] = block[:, at : at + owned]


def join_kernel(total, received, *outs):
    mine, side, half = row_place(total)
    for k, target in enumerate(outs):
        for i in range(half):
            block = total[(mine ^ k) * PACK + side * half + i] + received[k * half + i].astype(F32)
            write_block(target, i, block)


def halve_kernel(place, kept, *refs):
    *received, sent, own = refs
    side = (lax.axis_index("row") >> place) & 1
    low = 1 << place
    for n in range(sent.shape[0]):
        base = (n // low) * 2 * low + n % low
        for target, half in ((sent, 1 - side), (own, side)):
            value = kept[base + half * low]
            for part in received:
                value = value + part[base + half * low, : value.shape[0]].astype(F32)
            target[n] = value


def in_hbm(value):
    return pltpu.with_memory_space_constraint(value, pltpu.HBM)


def params(flops, size):
    return dict(
        compiler_params=pltpu.CompilerParams(vmem_limit_bytes=VMEM_LIMIT),
        cost_estimate=pl.CostEstimate(flops=flops, bytes_accessed=size, transcendentals=0),
    )


def body(
    slip, lowrank_u, lowrank_v, ranks, near_slot, near_blocks, velocity, theta, a_sigma, b_sigma
):
    groups, owners = lax.axis_size("col"), lax.axis_size("row")
    members = slip.shape[0]
    _, receivers, depth, _ = lowrank_v.shape
    owned = velocity.shape[1]
    _, count, _ = near_slot.shape
    n_groups = receivers // PACK
    per_group = owners // n_groups
    slots_by = jnp.swapaxes(near_slot, 1, 2)
    size = (lowrank_u.size + lowrank_v.size + near_blocks.size) // groups

    def col_swap(value, offset):
        return lax.ppermute(value, "col", [(i, i ^ offset) for i in range(groups)])

    def row_swap(value, offset):
        return lax.ppermute(value, "row", [(i, i ^ offset) for i in range(owners)])

    across = col_swap(slip, 2)
    sibling = col_swap(slip, 1)

    weights = (lowrank_u, lowrank_v, near_blocks)
    field = pltpu.VMEM(velocity.shape, F32)
    coeffs = pltpu.VMEM((receivers, members, depth), BF16)
    total_shape = pltpu.VMEM((receivers, members, LANES), F32)
    slots_smem = pltpu.SMEM(slots_by.shape, I32)
    total, u_later, v_later, near_later, kept, gain, shift, slots = pl.pallas_call(
        own_kernel,
        out_shape=[
            total_shape,
            *[pltpu.VMEM((3, *w.shape[1:]), BF16) for w in weights],
            pltpu.VMEM((groups, count, receivers * KMAX), F32), field, field, slots_smem,
        ],
        in_specs=[HBM_SPEC] * 10,
        out_specs=[VMEM_SPEC] * 7 + [SMEM_SPEC],
        scratch_shapes=[
            pltpu.VMEM(slip.shape, BF16),
            *[pltpu.VMEM(w.shape[1:], BF16) for w in weights],
            pltpu.VMEM(ranks.shape, I32), field, field,
            pltpu.VMEM((1, owned), F32), pltpu.VMEM((1, owned), F32),
            coeffs, pltpu.SemaphoreType.DMA((19,)),
        ],
        **params(2 * members * size, 8 * size),
    )(
        *map(
            in_hbm,
            (
                slip, *weights, ranks, slots_by, velocity, theta,
                a_sigma.reshape(1, owned), b_sigma.reshape(1, owned),
            ),
        )
    )
    across, total = lax.optimization_barrier((across, total))

    shards = (per_group // 2, members, owned)

    def later(offsets, slips, total):
        final = offsets[-1] == 3
        out_shape = [total_shape]
        if final:
            out_shape.append(pltpu.VMEM((3 * PACK // 2, members, LANES), BF16))
            out_shape += [pltpu.VMEM((shards[0], members + PAD, owned), BF16)] * 2
        return pl.pallas_call(
            functools.partial(later_kernel, offsets, final),
            out_shape=out_shape,
            in_specs=[VMEM_SPEC] * (len(slips) + 4) + [SMEM_SPEC, VMEM_SPEC],
            out_specs=[VMEM_SPEC] * len(out_shape),
            scratch_shapes=[coeffs],
            input_output_aliases={len(slips) + 5: 0},
            **params(2 * members * size * len(slips), 2 * size * len(slips)),
        )(*slips, u_later, v_later, near_later, kept, slots, total)

    beyond = col_swap(across, 1)
    (total,) = later((1, 2), (sibling, across), total)
    total, swapped, same, other = later((3,), (beyond,), total)
    swapped = row_swap(swapped, per_group // 2)
    other = row_swap(other, 3 * per_group + per_group // 2)
    same = row_swap(same, 3 * per_group)
    own, first, second = pl.pallas_call(
        join_kernel,
        out_shape=[pltpu.VMEM(shards, dtype) for dtype in (F32, BF16, BF16)],
        in_specs=[VMEM_SPEC] * 2,
        out_specs=[VMEM_SPEC] * 3,
        **params(0, 8 * swapped.size),
    )(total, swapped)
    received = [other, same, row_swap(second, 2 * per_group), row_swap(first, per_group)]
    for place in reversed(range(per_group.bit_length() - 2)):
        shape = (own.shape[0] // 2, members, owned)
        sent, own = pl.pallas_call(
            functools.partial(halve_kernel, place),
            out_shape=[pltpu.VMEM(shape, F32)] * 2,
            in_specs=[VMEM_SPEC] * (1 + len(received)),
            out_specs=[VMEM_SPEC] * 2,
            **params(0, 12 * own.size),
        )(own, *received)
        received = [row_swap(sent, 1 << place)]
    stress_rate = own[0]
    for part in received:
        stress_rate = stress_rate + part[0, :members].astype(F32)
    return (stress_rate, stress_rate * gain + shift)


def solution(mesh):
    placed = (
        P(None, ("col", "row")),
        P(None, "row", "col"),
        P(None, "col", "row", None),
        P(None, "row", "col"),
        P(None, "row", "col"),
        P(None, "row", "col"),
        P(None, ("col", "row")),
        P(None, ("col", "row")),
        P(("col", "row")),
        P(("col", "row")),
    )
    return jax.shard_map(
        body,
        mesh=mesh,
        in_specs=placed,
        out_specs=(P(None, ("col", "row")), P(None, ("col", "row"))),
        check_vma=False,
    )
```

```python
import functools

import jax
import jax.numpy as jnp
from jax import lax
from jax.experimental import pallas as pl
from jax.experimental.pallas import tpu as pltpu
from jax.sharding import PartitionSpec as P

BF16, F32, I32 = jnp.bfloat16, jnp.float32, jnp.int32
LANES = 128
KMAX = 32
PACK = LANES // KMAX
VMEM_LIMIT = 32 * 2**20
PAD = 16
HBM_SPEC = pl.BlockSpec(memory_space=pltpu.HBM)
VMEM_SPEC = pl.BlockSpec(memory_space=pltpu.VMEM)
SMEM_SPEC = pl.BlockSpec(memory_space=pltpu.SMEM)


def dot(left, right):
    return jnp.dot(left, right, preferred_element_type=F32)


def project(slip, u_ref, kept_ref, coeffs):
    count, width = kept_ref.shape
    place = lax.broadcasted_iota(I32, (1, LANES), 1) // KMAX
    for first in range(0, count, PACK):
        projected = []
        for b in range(first, first + PACK):
            rows = slice(b * LANES, (b + 1) * LANES)
            value = dot(slip[:, rows], u_ref[rows, :])
            projected.append(jnp.where(kept_ref[b : b + 1, :] > 0, value, 0.0))
        for g in range(width // LANES):
            turned = []
            for i, value in enumerate(projected):
                value = value[:, g * LANES : (g + 1) * LANES]
                value = pltpu.roll(value, i * KMAX, 1) if i else value
                turned.append(value.astype(BF16))
            for i in range(PACK):
                row = turned[-i % PACK]
                for c in range(1, PACK):
                    row = jnp.where(place == c, turned[(c - i) % PACK], row)
                coeffs[g * PACK + i, :, first * KMAX : (first + PACK) * KMAX] = row


def far_block(coeffs, v_ref, j):
    order = []
    for first in range(0, v_ref.shape[1] // KMAX, PACK):
        order += [first + (c - j) % PACK for c in range(PACK)]
    rows = [v_ref[j, b * KMAX : (b + 1) * KMAX, :] for b in order]
    return dot(coeffs[j], jnp.concatenate(rows, axis=0))


def add_near(slip, near_ref, slots, s, total):
    count = near_ref.shape[0] // LANES
    for b in range(count):
        rows = slice(b * LANES, (b + 1) * LANES)
        dense = dot(slip[:, rows], near_ref[rows, :])
        for slot in range(near_ref.shape[1] // LANES):
            total[slots[s, slot, b]] += dense[:, slot * LANES : (slot + 1) * LANES]


class Fetches:
    def __init__(self, sems):
        self.sems, self.used = sems, 0

    def __call__(self, source, target):
        copy = pltpu.make_async_copy(source, target, self.sems.at[self.used])
        self.used += 1
        copy.start()
        return copy


def wait_all(copies):
    for copy in copies:
        copy.wait()


def own_kernel(
    slip_hbm, u_hbm, v_hbm, near_hbm, ranks_hbm, slots_hbm, velocity_hbm, theta_hbm, a_hbm, b_hbm,
    total, u_out, v_out, near_out, kept, gain, shift, slots,
    slip, u_in, v_in, near_in, ranks, velocity, theta, a_sigma, b_sigma, coeffs, sems,
):
    me = lax.axis_index("col")
    fetch = Fetches(sems)
    small = [fetch(ranks_hbm, ranks), fetch(slots_hbm, slots)]
    mine = [
        fetch(slip_hbm, slip),
        fetch(u_hbm.at[me], u_in),
        fetch(v_hbm.at[me], v_in),
        fetch(near_hbm.at[me], near_in),
    ]
    fields = [
        fetch(velocity_hbm, velocity),
        fetch(theta_hbm, theta),
        fetch(a_hbm, a_sigma),
        fetch(b_hbm, b_sigma),
    ]
    later = []
    for i in range(3):
        s = me ^ (1 + i)
        later += [fetch(u_hbm.at[s], u_out.at[i]), fetch(near_hbm.at[s], near_out.at[i])]
        if i < 2:
            later.append(fetch(v_hbm.at[s], v_out.at[i]))
    wait_all(small)
    _, count, receivers = ranks.shape
    width = receivers * KMAX
    column = lax.broadcasted_iota(I32, (receivers, width), 1)
    spread = column // KMAX == lax.broadcasted_iota(I32, (receivers, width), 0)
    lane = lax.broadcasted_iota(I32, (1, width), 1)
    block, index = lane // KMAX, (lane % KMAX).astype(F32)
    for i in range(4):
        s = me ^ i
        wide = dot(ranks[s].astype(F32).astype(BF16), spread.astype(BF16))
        for b in range(count):
            keep = index < wide[b : b + 1, :]
            for slot in range(slots.shape[1]):
                keep = keep & (block != slots[s, slot, b])
            kept[i, b : b + 1, :] = keep.astype(F32)

    wait_all(mine)
    project(slip[...], u_in, kept.at[0], coeffs)
    for j in range(receivers):
        total[j] = far_block(coeffs, v_in, j)
    add_near(slip[...], near_in, slots, me, total)
    wait_all(fields)
    rate, state = velocity[...], theta[...]
    divisor = 1.0 / (a_sigma[...] / rate + 0.5)
    gain[...] = divisor
    shift[...] = -(b_sigma[...] * (1.0 - rate * state) / state) * divisor
    wait_all(later)


def middle_kernel(
    sibling, across, u_ref, v_ref, near_ref, kept, slots, start, v_hbm, total, v_last,
    coeffs, sem,
):
    me = lax.axis_index("col")
    copy = pltpu.make_async_copy(v_hbm.at[me ^ 3], v_last, sem)
    copy.start()

    @pl.when(me >= 0)
    def _():
        sections = ((1, sibling), (2, across))
        for i, slip in sections:
            project(slip[...], u_ref.at[i - 1], kept.at[i], coeffs.at[i - 1])
        for i, slip in sections:
            add_near(slip[...], near_ref.at[i - 1], slots, me ^ i, total)
        for j in range(total.shape[0]):
            total[j] += far_block(coeffs.at[0], v_ref.at[0], j) + far_block(
                coeffs.at[1], v_ref.at[1], j
            )

    copy.wait()


def last_kernel(
    beyond, u_ref, v_ref, near_ref, kept, slots, start, total, swapped, same, other, coeffs
):
    me = lax.axis_index("col")
    project(beyond[...], u_ref.at[2], kept.at[3], coeffs)
    add_near(beyond[...], near_ref.at[2], slots, me ^ 3, total)
    for j in range(total.shape[0]):
        total[j] += far_block(coeffs, v_ref, j)
    mine, side, half = row_place(total)
    for k in range(3):
        for i in range(half):
            block = total[(mine ^ k) * PACK + (1 - side) * half + i]
            swapped[k * half + i] = block.astype(swapped.dtype)
    for target, to_side in ((same, side), (other, 1 - side)):
        target[:, total.shape[1] :, :] = jnp.zeros_like(target[:, total.shape[1] :, :])
        for i in range(half):
            write_block(target, i, total[(mine ^ 3) * PACK + to_side * half + i])


def row_place(total):
    row, groups = lax.axis_index("row"), total.shape[0] // PACK
    per_group = lax.axis_size("row") // groups
    return row // per_group, row % per_group // (per_group // 2), PACK // 2


def write_block(target, i, block):
    owned, block = target.shape[2], block.astype(target.dtype)
    if owned >= LANES:
        n, at = divmod(i * LANES, owned)
        target[n, : block.shape[0], at : at + LANES] = block
    else:
        for at in range(0, LANES, owned):
            target[(i * LANES + at) // owned, : block.shape[0], :] = block[:, at : at + owned]


def join_kernel(total, received, *outs):
    mine, side, half = row_place(total)
    for k, target in enumerate(outs):
        for i in range(half):
            block = total[(mine ^ k) * PACK + side * half + i] + received[k * half + i].astype(F32)
            write_block(target, i, block)


def halve_kernel(place, kept, *refs):
    *received, sent, own = refs
    side = (lax.axis_index("row") >> place) & 1
    low = 1 << place
    for n in range(sent.shape[0]):
        base = (n // low) * 2 * low + n % low
        for target, half in ((sent, 1 - side), (own, side)):
            value = kept[base + half * low]
            for part in received:
                value = value + part[base + half * low, : value.shape[0]].astype(F32)
            target[n] = value


def in_hbm(value):
    return pltpu.with_memory_space_constraint(value, pltpu.HBM)


def params(flops, size):
    return dict(
        compiler_params=pltpu.CompilerParams(vmem_limit_bytes=VMEM_LIMIT),
        cost_estimate=pl.CostEstimate(flops=flops, bytes_accessed=size, transcendentals=0),
    )


def body(
    slip, lowrank_u, lowrank_v, ranks, near_slot, near_blocks, velocity, theta, a_sigma, b_sigma
):
    groups, owners = lax.axis_size("col"), lax.axis_size("row")
    members = slip.shape[0]
    _, receivers, depth, _ = lowrank_v.shape
    owned = velocity.shape[1]
    _, count, _ = near_slot.shape
    n_groups = receivers // PACK
    per_group = owners // n_groups
    slots_by = jnp.swapaxes(near_slot, 1, 2)
    size = (lowrank_u.size + lowrank_v.size + near_blocks.size) // groups

    def col_swap(value, offset):
        return lax.ppermute(value, "col", [(i, i ^ offset) for i in range(groups)])

    def row_swap(value, offset):
        return lax.ppermute(value, "row", [(i, i ^ offset) for i in range(owners)])

    across = col_swap(slip, 2)
    sibling = col_swap(slip, 1)

    weights = (lowrank_u, lowrank_v, near_blocks)
    field = pltpu.VMEM(velocity.shape, F32)
    coeffs = pltpu.VMEM((receivers, members, depth), BF16)
    total_shape = pltpu.VMEM((receivers, members, LANES), F32)
    slots_smem = pltpu.SMEM(slots_by.shape, I32)
    total, u_later, v_later, near_later, kept, gain, shift, slots = pl.pallas_call(
        own_kernel,
        out_shape=[
            total_shape,
            *[pltpu.VMEM((n, *w.shape[1:]), BF16) for n, w in zip((3, 2, 3), weights)],
            pltpu.VMEM((groups, count, receivers * KMAX), F32), field, field, slots_smem,
        ],
        in_specs=[HBM_SPEC] * 10,
        out_specs=[VMEM_SPEC] * 7 + [SMEM_SPEC],
        scratch_shapes=[
            pltpu.VMEM(slip.shape, BF16),
            *[pltpu.VMEM(w.shape[1:], BF16) for w in weights],
            pltpu.VMEM(ranks.shape, I32), field, field,
            pltpu.VMEM((1, owned), F32), pltpu.VMEM((1, owned), F32),
            coeffs, pltpu.SemaphoreType.DMA((18,)),
        ],
        **params(2 * members * size, 8 * size),
    )(
        *map(
            in_hbm,
            (
                slip, *weights, ranks, slots_by, velocity, theta,
                a_sigma.reshape(1, owned), b_sigma.reshape(1, owned),
            ),
        )
    )
    across, total = lax.optimization_barrier((across, total))

    shards = (per_group // 2, members, owned)

    beyond = col_swap(across, 1)
    total, v_last = pl.pallas_call(
        middle_kernel,
        out_shape=[total_shape, pltpu.VMEM(lowrank_v.shape[1:], BF16)],
        in_specs=[VMEM_SPEC] * 6 + [SMEM_SPEC, VMEM_SPEC, HBM_SPEC],
        out_specs=[VMEM_SPEC] * 2,
        scratch_shapes=[
            pltpu.VMEM((2, receivers, members, depth), BF16), pltpu.SemaphoreType.DMA
        ],
        input_output_aliases={7: 0},
        **params(4 * members * size, 4 * size),
    )(sibling, across, u_later, v_later, near_later, kept, slots, total, in_hbm(lowrank_v))
    total, swapped, same, other = pl.pallas_call(
        last_kernel,
        out_shape=[
            total_shape,
            pltpu.VMEM((3 * PACK // 2, members, LANES), BF16),
            *[pltpu.VMEM((shards[0], members + PAD, owned), BF16)] * 2,
        ],
        in_specs=[VMEM_SPEC] * 5 + [SMEM_SPEC, VMEM_SPEC],
        out_specs=[VMEM_SPEC] * 4,
        scratch_shapes=[coeffs],
        input_output_aliases={6: 0},
        **params(2 * members * size, 2 * size),
    )(beyond, u_later, v_last, near_later, kept, slots, total)
    swapped = row_swap(swapped, per_group // 2)
    other = row_swap(other, 3 * per_group + per_group // 2)
    same = row_swap(same, 3 * per_group)
    own, first, second = pl.pallas_call(
        join_kernel,
        out_shape=[pltpu.VMEM(shards, dtype) for dtype in (F32, BF16, BF16)],
        in_specs=[VMEM_SPEC] * 2,
        out_specs=[VMEM_SPEC] * 3,
        **params(0, 8 * swapped.size),
    )(total, swapped)
    received = [other, same, row_swap(second, 2 * per_group), row_swap(first, per_group)]
    for place in reversed(range(per_group.bit_length() - 2)):
        shape = (own.shape[0] // 2, members, owned)
        sent, own = pl.pallas_call(
            functools.partial(halve_kernel, place),
            out_shape=[pltpu.VMEM(shape, F32)] * 2,
            in_specs=[VMEM_SPEC] * (1 + len(received)),
            out_specs=[VMEM_SPEC] * 2,
            **params(0, 12 * own.size),
        )(own, *received)
        received = [row_swap(sent, 1 << place)]
    stress_rate = own[0]
    for part in received:
        stress_rate = stress_rate + part[0, :members].astype(F32)
    return (stress_rate, stress_rate * gain + shift)


def solution(mesh):
    placed = (
        P(None, ("col", "row")),
        P(None, "row", "col"),
        P(None, "col", "row", None),
        P(None, "row", "col"),
        P(None, "row", "col"),
        P(None, "row", "col"),
        P(None, ("col", "row")),
        P(None, ("col", "row")),
        P(("col", "row")),
        P(("col", "row")),
    )
    return jax.shard_map(
        body,
        mesh=mesh,
        in_specs=placed,
        out_specs=(P(None, ("col", "row")), P(None, ("col", "row"))),
        check_vma=False,
    )
```

```python
import functools

import jax
import jax.numpy as jnp
from jax import lax
from jax.experimental import pallas as pl
from jax.experimental.pallas import tpu as pltpu
from jax.sharding import PartitionSpec as P

BF16, F32, I32 = jnp.bfloat16, jnp.float32, jnp.int32
LANES = 128
KMAX = 32
PACK = LANES // KMAX
VMEM_LIMIT = 32 * 2**20
PAD = 16
TURNS = (0, 1, 3)
HBM_SPEC = pl.BlockSpec(memory_space=pltpu.HBM)
VMEM_SPEC = pl.BlockSpec(memory_space=pltpu.VMEM)
SMEM_SPEC = pl.BlockSpec(memory_space=pltpu.SMEM)


def dot(left, right):
    return jnp.dot(left, right, preferred_element_type=F32)


def project(slip, u_ref, kept_ref, coeffs):
    count, width = kept_ref.shape
    place = lax.broadcasted_iota(I32, (1, LANES), 1) // KMAX
    for first in range(0, count, PACK):
        projected = []
        for b in range(first, first + PACK):
            rows = slice(b * LANES, (b + 1) * LANES)
            value = dot(slip[:, rows], u_ref[rows, :])
            projected.append(jnp.where(kept_ref[b : b + 1, :] > 0, value, 0.0))
        for g in range(width // LANES):
            turned = []
            for i, value in enumerate(projected):
                value = value[:, g * LANES : (g + 1) * LANES]
                value = pltpu.roll(value, i * KMAX, 1) if i else value
                turned.append(value.astype(BF16))
            for i in range(PACK):
                row = turned[-i % PACK]
                for c in range(1, PACK):
                    row = jnp.where(place == c, turned[(c - i) % PACK], row)
                coeffs[g * PACK + i, :, first * KMAX : (first + PACK) * KMAX] = row


def far_block(coeffs, v_ref, j):
    order = []
    for first in range(0, v_ref.shape[1] // KMAX, PACK):
        order += [first + (c - j) % PACK for c in range(PACK)]
    rows = [v_ref[j, b * KMAX : (b + 1) * KMAX, :] for b in order]
    return dot(coeffs[j], jnp.concatenate(rows, axis=0))


def add_near(slip, near_ref, slots, s, total):
    count = near_ref.shape[0] // LANES
    for b in range(count):
        rows = slice(b * LANES, (b + 1) * LANES)
        dense = dot(slip[:, rows], near_ref[rows, :])
        for slot in range(near_ref.shape[1] // LANES):
            total[slots[s, slot, b]] += dense[:, slot * LANES : (slot + 1) * LANES]


class Fetches:
    def __init__(self, sems):
        self.sems, self.used = sems, 3

    def __call__(self, source, target, shared=None):
        own = self.used if shared is None else shared
        copy = pltpu.make_async_copy(source, target, self.sems.at[own])
        self.used += shared is None
        copy.start()
        return copy


def wait_all(copies):
    for copy in copies:
        copy.wait()


def own_kernel(
    slip_hbm, u_hbm, v_hbm, near_hbm, ranks_hbm, slots_hbm, velocity_hbm, theta_hbm, a_hbm, b_hbm,
    total, u_out, v_out, near_out, kept, gain, shift, slots,
    slip, u_in, v_in, near_in, ranks, velocity, theta, a_sigma, b_sigma, coeffs, sems,
):
    me = lax.axis_index("col")
    fetch = Fetches(sems)
    small = [fetch(ranks_hbm, ranks), fetch(slots_hbm, slots)]
    mine = [
        fetch(slip_hbm, slip),
        fetch(u_hbm.at[me], u_in),
        fetch(v_hbm.at[me], v_in),
        fetch(near_hbm.at[me], near_in),
    ]
    fields = [
        fetch(velocity_hbm, velocity),
        fetch(theta_hbm, theta),
        fetch(a_hbm, a_sigma),
        fetch(b_hbm, b_sigma),
    ]
    for i in range(3):
        s = me ^ (1 + i)
        fetch(u_hbm.at[s], u_out.at[i], 0)
        fetch(near_hbm.at[s], near_out.at[i], 1)
        if i < 2:
            fetch(v_hbm.at[s], v_out.at[i], 2)
    later = [
        pltpu.make_async_copy(whole, whole, sems.at[n])
        for n, whole in enumerate((u_out, near_out, v_out))
    ]
    @pl.when(me >= 0)
    def _():
        wait_all(small)
        _, count, receivers = ranks.shape
        width = receivers * KMAX
        column = lax.broadcasted_iota(I32, (receivers, width), 1)
        spread = column // KMAX == lax.broadcasted_iota(I32, (receivers, width), 0)
        lane = lax.broadcasted_iota(I32, (1, width), 1)
        block, index = lane // KMAX, (lane % KMAX).astype(F32)
        for i in range(4):
            s = me ^ i
            wide = dot(ranks[s].astype(F32).astype(BF16), spread.astype(BF16))
            for b in range(count):
                keep = index < wide[b : b + 1, :]
                for slot in range(slots.shape[1]):
                    keep = keep & (block != slots[s, slot, b])
                kept[i, b : b + 1, :] = keep.astype(F32)

        wait_all(mine)
        project(slip[...], u_in, kept.at[0], coeffs)
        for j in range(receivers):
            total[j] = far_block(coeffs, v_in, j)
        add_near(slip[...], near_in, slots, me, total)
        wait_all(fields)
        rate, state = velocity[...], theta[...]
        divisor = 1.0 / (a_sigma[...] / rate + 0.5)
        gain[...] = divisor
        shift[...] = -(b_sigma[...] * (1.0 - rate * state) / state) * divisor
        wait_all(later)


def middle_kernel(
    sibling, across, u_ref, v_ref, near_ref, kept, slots, start, v_hbm, total, v_last,
    coeffs, sem,
):
    me = lax.axis_index("col")
    copy = pltpu.make_async_copy(v_hbm.at[me ^ 3], v_last, sem)
    copy.start()

    @pl.when(me >= 0)
    def _():
        sections = ((1, sibling), (2, across))
        for i, slip in sections:
            project(slip[...], u_ref.at[i - 1], kept.at[i], coeffs.at[i - 1])
        for i, slip in sections:
            add_near(slip[...], near_ref.at[i - 1], slots, me ^ i, total)
        for j in range(total.shape[0]):
            total[j] += far_block(coeffs.at[0], v_ref.at[0], j) + far_block(
                coeffs.at[1], v_ref.at[1], j
            )

    copy.wait()


def last_kernel(
    beyond, u_ref, v_ref, near_ref, kept, slots, start, total, swapped, same, other, coeffs
):
    me = lax.axis_index("col")
    project(beyond[...], u_ref.at[2], kept.at[3], coeffs)
    add_near(beyond[...], near_ref.at[2], slots, me ^ 3, total)
    for j in range(total.shape[0]):
        total[j] += far_block(coeffs, v_ref, j)
    mine, side, half = row_place(total)
    for k in range(3):
        for i in range(half):
            block = total[turn(mine, TURNS[k]) * PACK + (1 - side) * half + i]
            swapped[k * half + i] = block.astype(swapped.dtype)
    for target, to_side in ((same, side), (other, 1 - side)):
        target[:, total.shape[1] :, :] = jnp.zeros_like(target[:, total.shape[1] :, :])
        for i in range(half):
            write_block(target, i, total[turn(mine, 2) * PACK + to_side * half + i])


def turn(group, by):
    return lax.rem(group + by, 4)


def row_place(total):
    row, groups = lax.axis_index("row"), total.shape[0] // PACK
    per_group = lax.axis_size("row") // groups
    return row // per_group, row % per_group // (per_group // 2), PACK // 2


def write_block(target, i, block):
    owned, block = target.shape[2], block.astype(target.dtype)
    if owned >= LANES:
        n, at = divmod(i * LANES, owned)
        target[n, : block.shape[0], at : at + LANES] = block
    else:
        for at in range(0, LANES, owned):
            target[(i * LANES + at) // owned, : block.shape[0], :] = block[:, at : at + owned]


def join_kernel(total, received, *outs):
    mine, side, half = row_place(total)
    for k, target in enumerate(outs):
        for i in range(half):
            block = total[turn(mine, TURNS[k]) * PACK + side * half + i] + received[k * half + i].astype(F32)
            write_block(target, i, block)


def halve_kernel(place, kept, *refs):
    *received, sent, own = refs
    side = (lax.axis_index("row") >> place) & 1
    low = 1 << place
    for n in range(sent.shape[0]):
        base = (n // low) * 2 * low + n % low
        for target, half in ((sent, 1 - side), (own, side)):
            value = kept[base + half * low]
            for part in received:
                value = value + part[base + half * low, : value.shape[0]].astype(F32)
            target[n] = value


def in_hbm(value):
    return pltpu.with_memory_space_constraint(value, pltpu.HBM)


def params(flops, size):
    return dict(
        compiler_params=pltpu.CompilerParams(vmem_limit_bytes=VMEM_LIMIT),
        cost_estimate=pl.CostEstimate(flops=flops, bytes_accessed=size, transcendentals=0),
    )


def body(
    slip, lowrank_u, lowrank_v, ranks, near_slot, near_blocks, velocity, theta, a_sigma, b_sigma
):
    groups, owners = lax.axis_size("col"), lax.axis_size("row")
    members = slip.shape[0]
    _, receivers, depth, _ = lowrank_v.shape
    owned = velocity.shape[1]
    _, count, _ = near_slot.shape
    n_groups = receivers // PACK
    per_group = owners // n_groups
    slots_by = jnp.swapaxes(near_slot, 1, 2)
    size = (lowrank_u.size + lowrank_v.size + near_blocks.size) // groups

    def col_swap(value, offset):
        return lax.ppermute(value, "col", [(i, i ^ offset) for i in range(groups)])

    def row_swap(value, offset):
        return lax.ppermute(value, "row", [(i, i ^ offset) for i in range(owners)])

    across = col_swap(slip, 2)
    sibling = col_swap(slip, 1)

    weights = (lowrank_u, lowrank_v, near_blocks)
    field = pltpu.VMEM(velocity.shape, F32)
    coeffs = pltpu.VMEM((receivers, members, depth), BF16)
    total_shape = pltpu.VMEM((receivers, members, LANES), F32)
    slots_smem = pltpu.SMEM(slots_by.shape, I32)
    total, u_later, v_later, near_later, kept, gain, shift, slots = pl.pallas_call(
        own_kernel,
        out_shape=[
            total_shape,
            *[pltpu.VMEM((n, *w.shape[1:]), BF16) for n, w in zip((3, 2, 3), weights)],
            pltpu.VMEM((groups, count, receivers * KMAX), F32), field, field, slots_smem,
        ],
        in_specs=[HBM_SPEC] * 10,
        out_specs=[VMEM_SPEC] * 7 + [SMEM_SPEC],
        scratch_shapes=[
            pltpu.VMEM(slip.shape, BF16),
            *[pltpu.VMEM(w.shape[1:], BF16) for w in weights],
            pltpu.VMEM(ranks.shape, I32), field, field,
            pltpu.VMEM((1, owned), F32), pltpu.VMEM((1, owned), F32),
            coeffs, pltpu.SemaphoreType.DMA((13,)),
        ],
        **params(2 * members * size, 8 * size),
    )(
        *map(
            in_hbm,
            (
                slip, *weights, ranks, slots_by, velocity, theta,
                a_sigma.reshape(1, owned), b_sigma.reshape(1, owned),
            ),
        )
    )
    across, total = lax.optimization_barrier((across, total))

    shards = (per_group // 2, members, owned)

    beyond = col_swap(across, 1)
    total, v_last = pl.pallas_call(
        middle_kernel,
        out_shape=[total_shape, pltpu.VMEM(lowrank_v.shape[1:], BF16)],
        in_specs=[VMEM_SPEC] * 6 + [SMEM_SPEC, VMEM_SPEC, HBM_SPEC],
        out_specs=[VMEM_SPEC] * 2,
        scratch_shapes=[
            pltpu.VMEM((2, receivers, members, depth), BF16), pltpu.SemaphoreType.DMA
        ],
        input_output_aliases={7: 0},
        **params(4 * members * size, 4 * size),
    )(sibling, across, u_later, v_later, near_later, kept, slots, total, in_hbm(lowrank_v))
    total, swapped, same, other = pl.pallas_call(
        last_kernel,
        out_shape=[
            total_shape,
            pltpu.VMEM((3 * PACK // 2, members, LANES), BF16),
            *[pltpu.VMEM((shards[0], members + PAD, owned), BF16)] * 2,
        ],
        in_specs=[VMEM_SPEC] * 5 + [SMEM_SPEC, VMEM_SPEC],
        out_specs=[VMEM_SPEC] * 4,
        scratch_shapes=[coeffs],
        input_output_aliases={6: 0},
        **params(2 * members * size, 2 * size),
    )(beyond, u_later, v_last, near_later, kept, slots, total)
    def group_send(value, by):
        return lax.ppermute(value, "row", [(i, (i + by * per_group) % owners) for i in range(owners)])

    swapped = row_swap(swapped, per_group // 2)
    other = row_swap(other, owners // 2 + per_group // 2)
    same = row_swap(same, owners // 2)
    own, first, second = pl.pallas_call(
        join_kernel,
        out_shape=[pltpu.VMEM(shards, dtype) for dtype in (F32, BF16, BF16)],
        in_specs=[VMEM_SPEC] * 2,
        out_specs=[VMEM_SPEC] * 3,
        **params(0, 8 * swapped.size),
    )(total, swapped)
    received = [other, same, group_send(first, 1), group_send(second, 3)]
    for place in reversed(range(per_group.bit_length() - 2)):
        shape = (own.shape[0] // 2, members, owned)
        sent, own = pl.pallas_call(
            functools.partial(halve_kernel, place),
            out_shape=[pltpu.VMEM(shape, F32)] * 2,
            in_specs=[VMEM_SPEC] * (1 + len(received)),
            out_specs=[VMEM_SPEC] * 2,
            **params(0, 12 * own.size),
        )(own, *received)
        received = [row_swap(sent, 1 << place)]
    stress_rate = own[0]
    for part in received:
        stress_rate = stress_rate + part[0, :members].astype(F32)
    return (stress_rate, stress_rate * gain + shift)


def solution(mesh):
    placed = (
        P(None, ("col", "row")),
        P(None, "row", "col"),
        P(None, "col", "row", None),
        P(None, "row", "col"),
        P(None, "row", "col"),
        P(None, "row", "col"),
        P(None, ("col", "row")),
        P(None, ("col", "row")),
        P(("col", "row")),
        P(("col", "row")),
    )
    return jax.shard_map(
        body,
        mesh=mesh,
        in_specs=placed,
        out_specs=(P(None, ("col", "row")), P(None, ("col", "row"))),
        check_vma=False,
    )
```

```python
import functools

import jax
import jax.numpy as jnp
from jax import lax
from jax.experimental import pallas as pl
from jax.experimental.pallas import tpu as pltpu
from jax.sharding import PartitionSpec as P

BF16, F32, I32 = jnp.bfloat16, jnp.float32, jnp.int32
LANES = 128
KMAX = 32
PACK = LANES // KMAX
VMEM_LIMIT = 32 * 2**20
TURNS = (0, 1, 3)
HBM_SPEC = pl.BlockSpec(memory_space=pltpu.HBM)
VMEM_SPEC = pl.BlockSpec(memory_space=pltpu.VMEM)
SMEM_SPEC = pl.BlockSpec(memory_space=pltpu.SMEM)


def dot(left, right):
    return jnp.dot(left, right, preferred_element_type=F32)


def project(slip, u_ref, kept_ref, coeffs):
    count, width = kept_ref.shape
    place = lax.broadcasted_iota(I32, (1, LANES), 1) // KMAX
    for first in range(0, count, PACK):
        projected = []
        for b in range(first, first + PACK):
            rows = slice(b * LANES, (b + 1) * LANES)
            value = dot(slip[:, rows], u_ref[rows, :])
            projected.append(jnp.where(kept_ref[b : b + 1, :] > 0, value, 0.0))
        for g in range(width // LANES):
            turned = []
            for i, value in enumerate(projected):
                value = value[:, g * LANES : (g + 1) * LANES]
                value = pltpu.roll(value, i * KMAX, 1) if i else value
                turned.append(value.astype(BF16))
            for i in range(PACK):
                row = turned[-i % PACK]
                for c in range(1, PACK):
                    row = jnp.where(place == c, turned[(c - i) % PACK], row)
                coeffs[g * PACK + i, :, first * KMAX : (first + PACK) * KMAX] = row


def far_block(coeffs, v_ref, j):
    order = []
    for first in range(0, v_ref.shape[1] // KMAX, PACK):
        order += [first + (c - j) % PACK for c in range(PACK)]
    rows = [v_ref[j, b * KMAX : (b + 1) * KMAX, :] for b in order]
    return dot(coeffs[j], jnp.concatenate(rows, axis=0))


def add_near(slip, near_ref, slots, s, total):
    count = near_ref.shape[0] // LANES
    for b in range(count):
        rows = slice(b * LANES, (b + 1) * LANES)
        dense = dot(slip[:, rows], near_ref[rows, :])
        for slot in range(near_ref.shape[1] // LANES):
            total[slots[s, slot, b]] += dense[:, slot * LANES : (slot + 1) * LANES]


class Fetches:
    def __init__(self, sems):
        self.sems, self.used = sems, 3

    def __call__(self, source, target, shared=None):
        own = self.used if shared is None else shared
        copy = pltpu.make_async_copy(source, target, self.sems.at[own])
        self.used += shared is None
        copy.start()
        return copy


def wait_all(copies):
    for copy in copies:
        copy.wait()


def own_kernel(
    slip_hbm, u_hbm, v_hbm, near_hbm, ranks_hbm, slots_hbm, velocity_hbm, theta_hbm, a_hbm, b_hbm,
    total, u_out, v_out, near_out, kept, gain, shift, slots,
    slip, u_in, v_in, near_in, ranks, velocity, theta, a_sigma, b_sigma, coeffs, sems,
):
    me = lax.axis_index("col")
    fetch = Fetches(sems)
    small = [fetch(ranks_hbm, ranks), fetch(slots_hbm, slots)]
    mine = [
        fetch(slip_hbm, slip),
        fetch(u_hbm.at[me], u_in),
        fetch(v_hbm.at[me], v_in),
        fetch(near_hbm.at[me], near_in),
    ]
    fields = [
        fetch(velocity_hbm, velocity),
        fetch(theta_hbm, theta),
        fetch(a_hbm, a_sigma),
        fetch(b_hbm, b_sigma),
    ]
    for i in range(3):
        s = me ^ (1 + i)
        fetch(u_hbm.at[s], u_out.at[i], 0)
        fetch(near_hbm.at[s], near_out.at[i], 1)
        if i < 2:
            fetch(v_hbm.at[s], v_out.at[i], 2)
    later = [
        pltpu.make_async_copy(whole, whole, sems.at[n])
        for n, whole in enumerate((u_out, near_out, v_out))
    ]
    @pl.when(me >= 0)
    def _():
        wait_all(small)
        _, count, receivers = ranks.shape
        width = receivers * KMAX
        column = lax.broadcasted_iota(I32, (receivers, width), 1)
        spread = column // KMAX == lax.broadcasted_iota(I32, (receivers, width), 0)
        lane = lax.broadcasted_iota(I32, (1, width), 1)
        block, index = lane // KMAX, (lane % KMAX).astype(F32)
        for i in range(4):
            s = me ^ i
            wide = dot(ranks[s].astype(F32).astype(BF16), spread.astype(BF16))
            for b in range(count):
                keep = index < wide[b : b + 1, :]
                for slot in range(slots.shape[1]):
                    keep = keep & (block != slots[s, slot, b])
                kept[i, b : b + 1, :] = keep.astype(F32)

        wait_all(mine)
        project(slip[...], u_in, kept.at[0], coeffs)
        for j in range(receivers):
            total[j] = far_block(coeffs, v_in, j)
        add_near(slip[...], near_in, slots, me, total)
        wait_all(fields)
        rate, state = velocity[...], theta[...]
        divisor = 1.0 / (a_sigma[...] / rate + 0.5)
        gain[...] = divisor
        shift[...] = -(b_sigma[...] * (1.0 - rate * state) / state) * divisor
        wait_all(later)


def middle_kernel(
    sibling, across, u_ref, v_ref, near_ref, kept, slots, start, v_hbm, total, v_last,
    coeffs, sem,
):
    me = lax.axis_index("col")
    copy = pltpu.make_async_copy(v_hbm.at[me ^ 3], v_last, sem)
    copy.start()

    @pl.when(me >= 0)
    def _():
        sections = ((1, sibling), (2, across))
        for i, slip in sections:
            project(slip[...], u_ref.at[i - 1], kept.at[i], coeffs.at[i - 1])
        for i, slip in sections:
            add_near(slip[...], near_ref.at[i - 1], slots, me ^ i, total)
        for j in range(total.shape[0]):
            total[j] += far_block(coeffs.at[0], v_ref.at[0], j) + far_block(
                coeffs.at[1], v_ref.at[1], j
            )

    copy.wait()


def last_kernel(
    beyond, u_ref, v_ref, near_ref, kept, slots, start, total, swapped, same, other, coeffs
):
    me = lax.axis_index("col")
    project(beyond[...], u_ref.at[2], kept.at[3], coeffs)
    add_near(beyond[...], near_ref.at[2], slots, me ^ 3, total)
    for j in range(total.shape[0]):
        total[j] += far_block(coeffs, v_ref, j)
    mine, side, half = row_place(total)
    for k in range(3):
        for i in range(half):
            block = total[turn(mine, TURNS[k]) * PACK + (1 - side) * half + i]
            swapped[k * half + i] = block.astype(swapped.dtype)
    for target, to_side in ((same, side), (other, 1 - side)):

        for i in range(half):
            write_block(target, i, total[turn(mine, 2) * PACK + to_side * half + i])


def turn(group, by):
    return lax.rem(group + by, 4)


def row_place(total):
    row, groups = lax.axis_index("row"), total.shape[0] // PACK
    per_group = lax.axis_size("row") // groups
    return row // per_group, row % per_group // (per_group // 2), PACK // 2


def write_block(target, i, block):
    owned, block = target.shape[2], block.astype(target.dtype)
    if owned >= LANES:
        n, at = divmod(i * LANES, owned)
        target[n, : block.shape[0], at : at + LANES] = block
    else:
        for at in range(0, LANES, owned):
            target[(i * LANES + at) // owned, : block.shape[0], :] = block[:, at : at + owned]


def join_kernel(total, received, *outs):
    mine, side, half = row_place(total)
    for k, target in enumerate(outs):
        for i in range(half):
            block = total[turn(mine, TURNS[k]) * PACK + side * half + i] + received[k * half + i].astype(F32)
            write_block(target, i, block)


def halve_kernel(place, kept, *refs):
    *received, sent, own = refs
    side = (lax.axis_index("row") >> place) & 1
    low = 1 << place
    for n in range(sent.shape[0]):
        base = (n // low) * 2 * low + n % low
        for target, half in ((sent, 1 - side), (own, side)):
            value = kept[base + half * low]
            for part in received:
                value = value + part[base + half * low, : value.shape[0]].astype(F32)
            target[n] = value


def in_hbm(value):
    return pltpu.with_memory_space_constraint(value, pltpu.HBM)


def params(flops, size):
    return dict(
        compiler_params=pltpu.CompilerParams(vmem_limit_bytes=VMEM_LIMIT),
        cost_estimate=pl.CostEstimate(flops=flops, bytes_accessed=size, transcendentals=0),
    )


def body(
    slip, lowrank_u, lowrank_v, ranks, near_slot, near_blocks, velocity, theta, a_sigma, b_sigma
):
    groups, owners = lax.axis_size("col"), lax.axis_size("row")
    members = slip.shape[0]
    _, receivers, depth, _ = lowrank_v.shape
    owned = velocity.shape[1]
    _, count, _ = near_slot.shape
    n_groups = receivers // PACK
    per_group = owners // n_groups
    slots_by = jnp.swapaxes(near_slot, 1, 2)
    size = (lowrank_u.size + lowrank_v.size + near_blocks.size) // groups

    def col_swap(value, offset):
        return lax.ppermute(value, "col", [(i, i ^ offset) for i in range(groups)])

    def row_swap(value, offset):
        return lax.ppermute(value, "row", [(i, i ^ offset) for i in range(owners)])

    across = col_swap(slip, 2)
    sibling = col_swap(slip, 1)

    weights = (lowrank_u, lowrank_v, near_blocks)
    field = pltpu.VMEM(velocity.shape, F32)
    coeffs = pltpu.VMEM((receivers, members, depth), BF16)
    total_shape = pltpu.VMEM((receivers, members, LANES), F32)
    slots_smem = pltpu.SMEM(slots_by.shape, I32)
    total, u_later, v_later, near_later, kept, gain, shift, slots = pl.pallas_call(
        own_kernel,
        out_shape=[
            total_shape,
            *[pltpu.VMEM((n, *w.shape[1:]), BF16) for n, w in zip((3, 2, 3), weights)],
            pltpu.VMEM((groups, count, receivers * KMAX), F32), field, field, slots_smem,
        ],
        in_specs=[HBM_SPEC] * 10,
        out_specs=[VMEM_SPEC] * 7 + [SMEM_SPEC],
        scratch_shapes=[
            pltpu.VMEM(slip.shape, BF16),
            *[pltpu.VMEM(w.shape[1:], BF16) for w in weights],
            pltpu.VMEM(ranks.shape, I32), field, field,
            pltpu.VMEM((1, owned), F32), pltpu.VMEM((1, owned), F32),
            coeffs, pltpu.SemaphoreType.DMA((13,)),
        ],
        **params(2 * members * size, 8 * size),
    )(
        *map(
            in_hbm,
            (
                slip, *weights, ranks, slots_by, velocity, theta,
                a_sigma.reshape(1, owned), b_sigma.reshape(1, owned),
            ),
        )
    )
    across, total = lax.optimization_barrier((across, total))

    shards = (per_group // 2, members, owned)

    beyond = col_swap(across, 1)
    total, v_last = pl.pallas_call(
        middle_kernel,
        out_shape=[total_shape, pltpu.VMEM(lowrank_v.shape[1:], BF16)],
        in_specs=[VMEM_SPEC] * 6 + [SMEM_SPEC, VMEM_SPEC, HBM_SPEC],
        out_specs=[VMEM_SPEC] * 2,
        scratch_shapes=[
            pltpu.VMEM((2, receivers, members, depth), BF16), pltpu.SemaphoreType.DMA
        ],
        input_output_aliases={7: 0},
        **params(4 * members * size, 4 * size),
    )(sibling, across, u_later, v_later, near_later, kept, slots, total, in_hbm(lowrank_v))
    total, swapped, same, other = pl.pallas_call(
        last_kernel,
        out_shape=[
            total_shape,
            pltpu.VMEM((3 * PACK // 2, members, LANES), BF16),
            *[pltpu.VMEM(shards, BF16)] * 2,
        ],
        in_specs=[VMEM_SPEC] * 5 + [SMEM_SPEC, VMEM_SPEC],
        out_specs=[VMEM_SPEC] * 4,
        scratch_shapes=[coeffs],
        input_output_aliases={6: 0},
        **params(2 * members * size, 2 * size),
    )(beyond, u_later, v_last, near_later, kept, slots, total)
    def group_send(value, by):
        return lax.ppermute(value, "row", [(i, (i + by * per_group) % owners) for i in range(owners)])

    swapped = row_swap(swapped, per_group // 2)
    other = row_swap(other, owners // 2 + per_group // 2)
    same = row_swap(same, owners // 2)
    own, first, second = pl.pallas_call(
        join_kernel,
        out_shape=[pltpu.VMEM(shards, dtype) for dtype in (F32, BF16, BF16)],
        in_specs=[VMEM_SPEC] * 2,
        out_specs=[VMEM_SPEC] * 3,
        **params(0, 8 * swapped.size),
    )(total, swapped)
    received = [other, same, group_send(first, 1), group_send(second, 3)]
    for place in reversed(range(per_group.bit_length() - 2)):
        shape = (own.shape[0] // 2, members, owned)
        sent, own = pl.pallas_call(
            functools.partial(halve_kernel, place),
            out_shape=[pltpu.VMEM(shape, F32)] * 2,
            in_specs=[VMEM_SPEC] * (1 + len(received)),
            out_specs=[VMEM_SPEC] * 2,
            **params(0, 12 * own.size),
        )(own, *received)
        received = [row_swap(sent, 1 << place)]
    stress_rate = own[0]
    for part in received:
        stress_rate = stress_rate + part[0, :members].astype(F32)
    return (stress_rate, stress_rate * gain + shift)


def solution(mesh):
    placed = (
        P(None, ("col", "row")),
        P(None, "row", "col"),
        P(None, "col", "row", None),
        P(None, "row", "col"),
        P(None, "row", "col"),
        P(None, "row", "col"),
        P(None, ("col", "row")),
        P(None, ("col", "row")),
        P(("col", "row")),
        P(("col", "row")),
    )
    return jax.shard_map(
        body,
        mesh=mesh,
        in_specs=placed,
        out_specs=(P(None, ("col", "row")), P(None, ("col", "row"))),
        check_vma=False,
    )
```

```python
import functools

import jax
import jax.numpy as jnp
from jax import lax
from jax.experimental import pallas as pl
from jax.experimental.pallas import tpu as pltpu
from jax.sharding import PartitionSpec as P

BF16, F32, I32 = jnp.bfloat16, jnp.float32, jnp.int32
LANES = 128
KMAX = 32
PACK = LANES // KMAX
VMEM_LIMIT = 32 * 2**20
HBM_SPEC = pl.BlockSpec(memory_space=pltpu.HBM)
VMEM_SPEC = pl.BlockSpec(memory_space=pltpu.VMEM)
SMEM_SPEC = pl.BlockSpec(memory_space=pltpu.SMEM)


def dot(left, right):
    return jnp.dot(left, right, preferred_element_type=F32)


def project(slip, u_ref, kept_ref, coeffs):
    count, width = kept_ref.shape
    place = lax.broadcasted_iota(I32, (1, LANES), 1) // KMAX
    for first in range(0, count, PACK):
        projected = []
        for b in range(first, first + PACK):
            rows = slice(b * LANES, (b + 1) * LANES)
            value = dot(slip[:, rows], u_ref[rows, :])
            projected.append(jnp.where(kept_ref[b : b + 1, :] > 0, value, 0.0))
        for g in range(width // LANES):
            turned = []
            for i, value in enumerate(projected):
                value = value[:, g * LANES : (g + 1) * LANES]
                value = pltpu.roll(value, i * KMAX, 1) if i else value
                turned.append(value.astype(BF16))
            for i in range(PACK):
                row = turned[-i % PACK]
                for c in range(1, PACK):
                    row = jnp.where(place == c, turned[(c - i) % PACK], row)
                coeffs[g * PACK + i, :, first * KMAX : (first + PACK) * KMAX] = row


def far_block(coeffs, v_ref, j):
    order = []
    for first in range(0, v_ref.shape[1] // KMAX, PACK):
        order += [first + (c - j) % PACK for c in range(PACK)]
    rows = [v_ref[j, b * KMAX : (b + 1) * KMAX, :] for b in order]
    return dot(coeffs[j], jnp.concatenate(rows, axis=0))


def add_near(slip, near_ref, slots, s, total):
    count = near_ref.shape[0] // LANES
    for b in range(count):
        rows = slice(b * LANES, (b + 1) * LANES)
        dense = dot(slip[:, rows], near_ref[rows, :])
        for slot in range(near_ref.shape[1] // LANES):
            total[slots[s, slot, b]] += dense[:, slot * LANES : (slot + 1) * LANES]


class Fetches:
    def __init__(self, sems, used):
        self.sems, self.used = sems, used

    def plan(self, source, target, shared=None):
        own = self.used if shared is None else shared
        self.used += shared is None
        return pltpu.make_async_copy(source, target, self.sems.at[own])

    def __call__(self, source, target, shared=None):
        copy = self.plan(source, target, shared)
        copy.start()
        return copy


def last_copies(me, fetch, u_hbm, near_hbm, u_last, near_last):
    return [
        fetch.plan(u_hbm.at[me ^ 3], u_last),
        fetch.plan(near_hbm.at[me ^ 3], near_last),
    ]


def start_all(copies):
    for copy in copies:
        copy.start()


def wait_all(copies):
    for copy in copies:
        copy.wait()


def own_kernel(
    slip_hbm, u_hbm, v_hbm, near_hbm, ranks_hbm, slots_hbm, velocity_hbm, theta_hbm, a_hbm, b_hbm,
    total, u_out, v_out, near_out, u_last, near_last, kept, gain, shift, slots,
    slip, u_in, v_in, near_in, ranks, velocity, theta, a_sigma, b_sigma, coeffs, sems,
):
    me = lax.axis_index("col")
    fetch = Fetches(sems, 3)
    small = [fetch(ranks_hbm, ranks), fetch(slots_hbm, slots)]
    mine = [
        fetch(slip_hbm, slip),
        fetch(u_hbm.at[me], u_in),
        fetch(v_hbm.at[me], v_in),
        fetch(near_hbm.at[me], near_in),
    ]
    fields = [
        fetch(velocity_hbm, velocity),
        fetch(theta_hbm, theta),
        fetch(a_hbm, a_sigma),
        fetch(b_hbm, b_sigma),
    ]
    for i in range(2):
        s = me ^ (1 + i)
        fetch(u_hbm.at[s], u_out.at[i], 0)
        fetch(near_hbm.at[s], near_out.at[i], 1)
        fetch(v_hbm.at[s], v_out.at[i], 2)
    later = [
        pltpu.make_async_copy(whole, whole, sems.at[n])
        for n, whole in enumerate((u_out, near_out, v_out))
    ]
    last = last_copies(me, fetch, u_hbm, near_hbm, u_last, near_last)
    pl.when(me % 2 == 0)(lambda: start_all(last))
    @pl.when(me >= 0)
    def _():
        wait_all(small)
        _, count, receivers = ranks.shape
        width = receivers * KMAX
        column = lax.broadcasted_iota(I32, (receivers, width), 1)
        spread = column // KMAX == lax.broadcasted_iota(I32, (receivers, width), 0)
        lane = lax.broadcasted_iota(I32, (1, width), 1)
        block, index = lane // KMAX, (lane % KMAX).astype(F32)
        for i in range(4):
            s = me ^ i
            wide = dot(ranks[s].astype(F32).astype(BF16), spread.astype(BF16))
            for b in range(count):
                keep = index < wide[b : b + 1, :]
                for slot in range(slots.shape[1]):
                    keep = keep & (block != slots[s, slot, b])
                kept[i, b : b + 1, :] = keep.astype(F32)

        wait_all(mine)
        project(slip[...], u_in, kept.at[0], coeffs)
        for j in range(receivers):
            total[j] = far_block(coeffs, v_in, j)
        add_near(slip[...], near_in, slots, me, total)
        wait_all(fields)
        rate, state = velocity[...], theta[...]
        divisor = 1.0 / (a_sigma[...] / rate + 0.5)
        gain[...] = divisor
        shift[...] = -(b_sigma[...] * (1.0 - rate * state) / state) * divisor
        wait_all(later)

    pl.when(me % 2 == 0)(lambda: wait_all(last))


def middle_kernel(
    sibling, across, u_ref, v_ref, near_ref, kept, slots, start, u_start, near_start,
    u_hbm, v_hbm, near_hbm, total, u_last, near_last, v_last, coeffs, sems,
):
    me = lax.axis_index("col")
    fetch = Fetches(sems, 0)
    copy = fetch(v_hbm.at[me ^ 3], v_last)
    last = last_copies(me, fetch, u_hbm, near_hbm, u_last, near_last)
    pl.when(me % 2 != 0)(lambda: start_all(last))

    @pl.when(me >= 0)
    def _():
        sections = ((1, sibling), (2, across))
        for i, slip in sections:
            project(slip[...], u_ref.at[i - 1], kept.at[i], coeffs.at[i - 1])
        for i, slip in sections:
            add_near(slip[...], near_ref.at[i - 1], slots, me ^ i, total)
        for j in range(total.shape[0]):
            total[j] += far_block(coeffs.at[0], v_ref.at[0], j) + far_block(
                coeffs.at[1], v_ref.at[1], j
            )

    copy.wait()
    pl.when(me % 2 != 0)(lambda: wait_all(last))


def last_kernel(
    beyond, u_ref, v_ref, near_ref, kept, slots, start, total, swapped, same, other, coeffs
):
    me = lax.axis_index("col")
    project(beyond[...], u_ref, kept.at[3], coeffs)
    add_near(beyond[...], near_ref, slots, me ^ 3, total)
    for j in range(total.shape[0]):
        total[j] += far_block(coeffs, v_ref, j)
    half = PACK // 2
    swap, direct, _ = routes(total)
    for k, first in enumerate(swap):
        for i in range(half):
            swapped[k * half + i] = total[first + i].astype(swapped.dtype)
    for target, first in zip((other, same), direct):
        for i in range(half):
            write_block(target, i, total[first + i])


def routes(total):
    even = lax.axis_index("col") % 2 == 0
    mine, side, half = row_place(total)

    def at(by, there, bits, other):
        group = jnp.where(even, turn(mine, by), mine ^ bits)
        return group * PACK + jnp.where(even, there, other) * half

    far = 1 - side
    swap = [at(0, far, 1, side), at(1, far, 1, far), at(3, far, 3, side)]
    direct = [at(2, far, 3, far), at(2, side, 2, far)]
    join = [at(0, side, 0, side), at(1, side, 0, far), at(3, side, 2, side)]
    return swap, direct, join


def turn(group, by):
    return lax.rem(group + by, 4)


def row_place(total):
    row, groups = lax.axis_index("row"), total.shape[0] // PACK
    per_group = lax.axis_size("row") // groups
    return row // per_group, row % per_group // (per_group // 2), PACK // 2


def write_block(target, i, block):
    owned, block = target.shape[2], block.astype(target.dtype)
    if owned >= LANES:
        n, at = divmod(i * LANES, owned)
        target[n, : block.shape[0], at : at + LANES] = block
    else:
        for at in range(0, LANES, owned):
            target[(i * LANES + at) // owned, : block.shape[0], :] = block[:, at : at + owned]


def join_kernel(total, received, *outs):
    half = PACK // 2
    _, _, join = routes(total)
    for k, (target, first) in enumerate(zip(outs, join)):
        for i in range(half):
            write_block(target, i, total[first + i] + received[k * half + i].astype(F32))


def halve_kernel(place, kept, *refs):
    *received, sent, own = refs
    side = (lax.axis_index("row") >> place) & 1
    low = 1 << place
    for n in range(sent.shape[0]):
        base = (n // low) * 2 * low + n % low
        for target, half in ((sent, 1 - side), (own, side)):
            value = kept[base + half * low]
            for part in received:
                value = value + part[base + half * low, : value.shape[0]].astype(F32)
            target[n] = value


def in_hbm(value):
    return pltpu.with_memory_space_constraint(value, pltpu.HBM)


def params(flops, size):
    return dict(
        compiler_params=pltpu.CompilerParams(vmem_limit_bytes=VMEM_LIMIT),
        cost_estimate=pl.CostEstimate(flops=flops, bytes_accessed=size, transcendentals=0),
    )


def body(
    slip, lowrank_u, lowrank_v, ranks, near_slot, near_blocks, velocity, theta, a_sigma, b_sigma
):
    groups, owners = lax.axis_size("col"), lax.axis_size("row")
    members = slip.shape[0]
    _, receivers, depth, _ = lowrank_v.shape
    owned = velocity.shape[1]
    _, count, _ = near_slot.shape
    n_groups = receivers // PACK
    per_group = owners // n_groups
    slots_by = jnp.swapaxes(near_slot, 1, 2)
    size = (lowrank_u.size + lowrank_v.size + near_blocks.size) // groups

    def col_swap(value, offset):
        return lax.ppermute(value, "col", [(i, i ^ offset) for i in range(groups)])

    def row_swap(value, offset):
        return lax.ppermute(value, "row", [(i, i ^ offset) for i in range(owners)])

    across = col_swap(slip, 2)
    sibling = col_swap(slip, 1)

    weights = (lowrank_u, lowrank_v, near_blocks)
    field = pltpu.VMEM(velocity.shape, F32)
    last_shapes = [pltpu.VMEM(w.shape[1:], BF16) for w in (lowrank_u, near_blocks)]
    coeffs = pltpu.VMEM((receivers, members, depth), BF16)
    total_shape = pltpu.VMEM((receivers, members, LANES), F32)
    slots_smem = pltpu.SMEM(slots_by.shape, I32)
    total, u_later, v_later, near_later, u_last, near_last, kept, gain, shift, slots = pl.pallas_call(
        own_kernel,
        out_shape=[
            total_shape,
            *[pltpu.VMEM((2, *w.shape[1:]), BF16) for w in weights],
            *last_shapes,
            pltpu.VMEM((groups, count, receivers * KMAX), F32), field, field, slots_smem,
        ],
        in_specs=[HBM_SPEC] * 10,
        out_specs=[VMEM_SPEC] * 9 + [SMEM_SPEC],
        scratch_shapes=[
            pltpu.VMEM(slip.shape, BF16),
            *[pltpu.VMEM(w.shape[1:], BF16) for w in weights],
            pltpu.VMEM(ranks.shape, I32), field, field,
            pltpu.VMEM((1, owned), F32), pltpu.VMEM((1, owned), F32),
            coeffs, pltpu.SemaphoreType.DMA((15,)),
        ],
        **params(2 * members * size, 8 * size),
    )(
        *map(
            in_hbm,
            (
                slip, *weights, ranks, slots_by, velocity, theta,
                a_sigma.reshape(1, owned), b_sigma.reshape(1, owned),
            ),
        )
    )
    across, total = lax.optimization_barrier((across, total))

    shards = (per_group // 2, members, owned)

    beyond = col_swap(across, 1)
    total, u_last, near_last, v_last = pl.pallas_call(
        middle_kernel,
        out_shape=[total_shape, *last_shapes, pltpu.VMEM(lowrank_v.shape[1:], BF16)],
        in_specs=[VMEM_SPEC] * 6 + [SMEM_SPEC] + [VMEM_SPEC] * 3 + [HBM_SPEC] * 3,
        out_specs=[VMEM_SPEC] * 4,
        scratch_shapes=[
            pltpu.VMEM((2, receivers, members, depth), BF16), pltpu.SemaphoreType.DMA((3,))
        ],
        input_output_aliases={7: 0, 8: 1, 9: 2},
        **params(4 * members * size, 4 * size),
    )(
        sibling, across, u_later, v_later, near_later, kept, slots, total, u_last, near_last,
        *map(in_hbm, weights),
    )
    total, swapped, same, other = pl.pallas_call(
        last_kernel,
        out_shape=[
            total_shape,
            pltpu.VMEM((3 * PACK // 2, members, LANES), BF16),
            *[pltpu.VMEM(shards, BF16)] * 2,
        ],
        in_specs=[VMEM_SPEC] * 5 + [SMEM_SPEC, VMEM_SPEC],
        out_specs=[VMEM_SPEC] * 4,
        scratch_shapes=[coeffs],
        input_output_aliases={6: 0},
        **params(2 * members * size, 2 * size),
    )(beyond, u_last, v_last, near_last, kept, slots, total)
    def send(value, by, bits, halves):
        pairs = []
        for i in range(groups * owners):
            col, row = divmod(i, owners)
            group, place = divmod(row, per_group)
            group = group ^ bits if col % 2 else (group + by) % n_groups
            place ^= per_group // 2 if halves[col % 2] else 0
            pairs.append((i, (col * n_groups + group) * per_group + place))
        return lax.ppermute(value, ("col", "row"), pairs)

    swapped = send(swapped, 0, 1, (True, False))
    other = send(other, 2, 3, (True, True))
    same = send(same, 2, 2, (False, True))
    own, first, second = pl.pallas_call(
        join_kernel,
        out_shape=[pltpu.VMEM(shards, dtype) for dtype in (F32, BF16, BF16)],
        in_specs=[VMEM_SPEC] * 2,
        out_specs=[VMEM_SPEC] * 3,
        **params(0, 8 * swapped.size),
    )(total, swapped)
    received = [
        other, same, send(first, 1, 0, (False, True)), send(second, 3, 2, (False, False))
    ]
    for place in reversed(range(per_group.bit_length() - 2)):
        shape = (own.shape[0] // 2, members, owned)
        sent, own = pl.pallas_call(
            functools.partial(halve_kernel, place),
            out_shape=[pltpu.VMEM(shape, F32)] * 2,
            in_specs=[VMEM_SPEC] * (1 + len(received)),
            out_specs=[VMEM_SPEC] * 2,
            **params(0, 12 * own.size),
        )(own, *received)
        received = [row_swap(sent, 1 << place)]
    stress_rate = own[0]
    for part in received:
        stress_rate = stress_rate + part[0, :members].astype(F32)
    return (stress_rate, stress_rate * gain + shift)


def solution(mesh):
    placed = (
        P(None, ("col", "row")),
        P(None, "row", "col"),
        P(None, "col", "row", None),
        P(None, "row", "col"),
        P(None, "row", "col"),
        P(None, "row", "col"),
        P(None, ("col", "row")),
        P(None, ("col", "row")),
        P(("col", "row")),
        P(("col", "row")),
    )
    return jax.shard_map(
        body,
        mesh=mesh,
        in_specs=placed,
        out_specs=(P(None, ("col", "row")), P(None, ("col", "row"))),
        check_vma=False,
    )
```

```python
import functools

import jax
import jax.numpy as jnp
from jax import lax
from jax.experimental import pallas as pl
from jax.experimental.pallas import tpu as pltpu
from jax.sharding import PartitionSpec as P

BF16, F32, I32 = jnp.bfloat16, jnp.float32, jnp.int32
LANES = 128
KMAX = 32
PACK = LANES // KMAX
VMEM_LIMIT = 32 * 2**20
HBM_SPEC = pl.BlockSpec(memory_space=pltpu.HBM)
VMEM_SPEC = pl.BlockSpec(memory_space=pltpu.VMEM)
SMEM_SPEC = pl.BlockSpec(memory_space=pltpu.SMEM)


def dot(left, right):
    return jnp.dot(left, right, preferred_element_type=F32)


def project(slip, u_ref, kept_ref, coeffs):
    count, width = kept_ref.shape
    place = lax.broadcasted_iota(I32, (1, LANES), 1) // KMAX
    for first in range(0, count, PACK):
        projected = []
        for b in range(first, first + PACK):
            rows = slice(b * LANES, (b + 1) * LANES)
            value = dot(slip[:, rows], u_ref[rows, :])
            projected.append(jnp.where(kept_ref[b : b + 1, :] > 0, value, 0.0))
        for g in range(width // LANES):
            turned = []
            for i, value in enumerate(projected):
                value = value[:, g * LANES : (g + 1) * LANES]
                value = pltpu.roll(value, i * KMAX, 1) if i else value
                turned.append(value.astype(BF16))
            for i in range(PACK):
                row = turned[-i % PACK]
                for c in range(1, PACK):
                    row = jnp.where(place == c, turned[(c - i) % PACK], row)
                coeffs[g * PACK + i, :, first * KMAX : (first + PACK) * KMAX] = row


def far_block(coeffs, v_ref, j):
    order = []
    for first in range(0, v_ref.shape[1] // KMAX, PACK):
        order += [first + (c - j) % PACK for c in range(PACK)]
    rows = [v_ref[j, b * KMAX : (b + 1) * KMAX, :] for b in order]
    return dot(coeffs[j], jnp.concatenate(rows, axis=0))


def add_near(slip, near_ref, slots, s, total):
    count = near_ref.shape[0] // LANES
    for b in range(count):
        rows = slice(b * LANES, (b + 1) * LANES)
        dense = dot(slip[:, rows], near_ref[rows, :])
        for slot in range(near_ref.shape[1] // LANES):
            total[slots[s, slot, b]] += dense[:, slot * LANES : (slot + 1) * LANES]


class Fetches:
    def __init__(self, sems, used):
        self.sems, self.used = sems, used

    def plan(self, source, target, shared=None):
        own = self.used if shared is None else shared
        self.used += shared is None
        return pltpu.make_async_copy(source, target, self.sems.at[own])

    def __call__(self, source, target, shared=None):
        copy = self.plan(source, target, shared)
        copy.start()
        return copy


def last_copies(me, fetch, u_hbm, near_hbm, u_last, near_last):
    return [
        fetch.plan(u_hbm.at[me ^ 3], u_last),
        fetch.plan(near_hbm.at[me ^ 3], near_last),
    ]


def wait_all(copies):
    for copy in copies:
        copy.wait()


def own_kernel(
    slip_hbm, u_hbm, v_hbm, near_hbm, ranks_hbm, slots_hbm, velocity_hbm, theta_hbm, a_hbm, b_hbm,
    total, u_out, v_out, near_out, u_last, near_last, kept, gain, shift, slots,
    slip, u_in, v_in, near_in, ranks, velocity, theta, a_sigma, b_sigma, coeffs, sems,
):
    me = lax.axis_index("col")
    fetch = Fetches(sems, 3)
    small = [fetch(ranks_hbm, ranks), fetch(slots_hbm, slots)]
    mine = [
        fetch(slip_hbm, slip),
        fetch(u_hbm.at[me], u_in),
        fetch(v_hbm.at[me], v_in),
        fetch(near_hbm.at[me], near_in),
    ]
    fields = [
        fetch(velocity_hbm, velocity),
        fetch(theta_hbm, theta),
        fetch(a_hbm, a_sigma),
        fetch(b_hbm, b_sigma),
    ]
    for i in range(2):
        s = me ^ (1 + i)
        fetch(u_hbm.at[s], u_out.at[i], 0)
        fetch(near_hbm.at[s], near_out.at[i], 1)
        fetch(v_hbm.at[s], v_out.at[i], 2)
    later = [
        pltpu.make_async_copy(whole, whole, sems.at[n])
        for n, whole in enumerate((u_out, near_out, v_out))
    ]
    last = last_copies(me, fetch, u_hbm, near_hbm, u_last, near_last)
    last[0].start()
    pl.when(me % 2 == 0)(last[1].start)
    @pl.when(me >= 0)
    def _():
        wait_all(small)
        _, count, receivers = ranks.shape
        width = receivers * KMAX
        column = lax.broadcasted_iota(I32, (receivers, width), 1)
        spread = column // KMAX == lax.broadcasted_iota(I32, (receivers, width), 0)
        lane = lax.broadcasted_iota(I32, (1, width), 1)
        block, index = lane // KMAX, (lane % KMAX).astype(F32)
        for i in range(4):
            s = me ^ i
            wide = dot(ranks[s].astype(F32).astype(BF16), spread.astype(BF16))
            for b in range(count):
                keep = index < wide[b : b + 1, :]
                for slot in range(slots.shape[1]):
                    keep = keep & (block != slots[s, slot, b])
                kept[i, b : b + 1, :] = keep.astype(F32)

        wait_all(mine)
        project(slip[...], u_in, kept.at[0], coeffs)
        for j in range(receivers):
            total[j] = far_block(coeffs, v_in, j)
        add_near(slip[...], near_in, slots, me, total)
        wait_all(fields)
        rate, state = velocity[...], theta[...]
        divisor = 1.0 / (a_sigma[...] / rate + 0.5)
        gain[...] = divisor
        shift[...] = -(b_sigma[...] * (1.0 - rate * state) / state) * divisor
        wait_all(later)

    last[0].wait()
    pl.when(me % 2 == 0)(last[1].wait)


def middle_kernel(
    sibling, across, u_ref, v_ref, near_ref, kept, slots, start, u_start, near_start,
    u_hbm, v_hbm, near_hbm, total, u_last, near_last, v_last, coeffs, sems,
):
    me = lax.axis_index("col")
    fetch = Fetches(sems, 0)
    copy = fetch(v_hbm.at[me ^ 3], v_last)
    last = last_copies(me, fetch, u_hbm, near_hbm, u_last, near_last)
    pl.when(me % 2 != 0)(last[1].start)

    @pl.when(me >= 0)
    def _():
        sections = ((1, sibling), (2, across))
        for i, slip in sections:
            project(slip[...], u_ref.at[i - 1], kept.at[i], coeffs.at[i - 1])
        for i, slip in sections:
            add_near(slip[...], near_ref.at[i - 1], slots, me ^ i, total)
        for j in range(total.shape[0]):
            total[j] += far_block(coeffs.at[0], v_ref.at[0], j) + far_block(
                coeffs.at[1], v_ref.at[1], j
            )

    copy.wait()
    pl.when(me % 2 != 0)(last[1].wait)


def last_kernel(
    beyond, u_ref, v_ref, near_ref, kept, slots, start, total, swapped, same, other, coeffs
):
    me = lax.axis_index("col")
    project(beyond[...], u_ref, kept.at[3], coeffs)
    add_near(beyond[...], near_ref, slots, me ^ 3, total)
    for j in range(total.shape[0]):
        total[j] += far_block(coeffs, v_ref, j)
    half = PACK // 2
    swap, direct, _ = routes(total)
    for k, first in enumerate(swap):
        for i in range(half):
            swapped[k * half + i] = total[first + i].astype(swapped.dtype)
    for target, first in zip((other, same), direct):
        for i in range(half):
            write_block(target, i, total[first + i])


def routes(total):
    even = lax.axis_index("col") % 2 == 0
    mine, side, half = row_place(total)

    def at(by, there, bits, other):
        group = jnp.where(even, turn(mine, by), mine ^ bits)
        return group * PACK + jnp.where(even, there, other) * half

    far = 1 - side
    swap = [at(0, far, 2, side), at(1, far, 2, far), at(3, far, 3, side)]
    direct = [at(2, far, 3, far), at(2, side, 1, far)]
    join = [at(0, side, 0, side), at(1, side, 0, far), at(3, side, 1, side)]
    return swap, direct, join


def turn(group, by):
    return lax.rem(group + by, 4)


def row_place(total):
    row, groups = lax.axis_index("row"), total.shape[0] // PACK
    per_group = lax.axis_size("row") // groups
    return row // per_group, row % per_group // (per_group // 2), PACK // 2


def write_block(target, i, block):
    owned, block = target.shape[2], block.astype(target.dtype)
    if owned >= LANES:
        n, at = divmod(i * LANES, owned)
        target[n, : block.shape[0], at : at + LANES] = block
    else:
        for at in range(0, LANES, owned):
            target[(i * LANES + at) // owned, : block.shape[0], :] = block[:, at : at + owned]


def join_kernel(total, received, *outs):
    half = PACK // 2
    _, _, join = routes(total)
    for k, (target, first) in enumerate(zip(outs, join)):
        for i in range(half):
            write_block(target, i, total[first + i] + received[k * half + i].astype(F32))


def halve_kernel(place, kept, *refs):
    *received, sent, own = refs
    side = (lax.axis_index("row") >> place) & 1
    low = 1 << place
    for n in range(sent.shape[0]):
        base = (n // low) * 2 * low + n % low
        for target, half in ((sent, 1 - side), (own, side)):
            value = kept[base + half * low]
            for part in received:
                value = value + part[base + half * low, : value.shape[0]].astype(F32)
            target[n] = value


def in_hbm(value):
    return pltpu.with_memory_space_constraint(value, pltpu.HBM)


def params(flops, size):
    return dict(
        compiler_params=pltpu.CompilerParams(vmem_limit_bytes=VMEM_LIMIT),
        cost_estimate=pl.CostEstimate(flops=flops, bytes_accessed=size, transcendentals=0),
    )


def body(
    slip, lowrank_u, lowrank_v, ranks, near_slot, near_blocks, velocity, theta, a_sigma, b_sigma
):
    groups, owners = lax.axis_size("col"), lax.axis_size("row")
    members = slip.shape[0]
    _, receivers, depth, _ = lowrank_v.shape
    owned = velocity.shape[1]
    _, count, _ = near_slot.shape
    n_groups = receivers // PACK
    per_group = owners // n_groups
    slots_by = jnp.swapaxes(near_slot, 1, 2)
    size = (lowrank_u.size + lowrank_v.size + near_blocks.size) // groups

    def col_swap(value, offset):
        return lax.ppermute(value, "col", [(i, i ^ offset) for i in range(groups)])

    def row_swap(value, offset):
        return lax.ppermute(value, "row", [(i, i ^ offset) for i in range(owners)])

    across = col_swap(slip, 2)
    sibling = col_swap(slip, 1)

    weights = (lowrank_u, lowrank_v, near_blocks)
    field = pltpu.VMEM(velocity.shape, F32)
    last_shapes = [pltpu.VMEM(w.shape[1:], BF16) for w in (lowrank_u, near_blocks)]
    coeffs = pltpu.VMEM((receivers, members, depth), BF16)
    total_shape = pltpu.VMEM((receivers, members, LANES), F32)
    slots_smem = pltpu.SMEM(slots_by.shape, I32)
    total, u_later, v_later, near_later, u_last, near_last, kept, gain, shift, slots = pl.pallas_call(
        own_kernel,
        out_shape=[
            total_shape,
            *[pltpu.VMEM((2, *w.shape[1:]), BF16) for w in weights],
            *last_shapes,
            pltpu.VMEM((groups, count, receivers * KMAX), F32), field, field, slots_smem,
        ],
        in_specs=[HBM_SPEC] * 10,
        out_specs=[VMEM_SPEC] * 9 + [SMEM_SPEC],
        scratch_shapes=[
            pltpu.VMEM(slip.shape, BF16),
            *[pltpu.VMEM(w.shape[1:], BF16) for w in weights],
            pltpu.VMEM(ranks.shape, I32), field, field,
            pltpu.VMEM((1, owned), F32), pltpu.VMEM((1, owned), F32),
            coeffs, pltpu.SemaphoreType.DMA((15,)),
        ],
        **params(2 * members * size, 8 * size),
    )(
        *map(
            in_hbm,
            (
                slip, *weights, ranks, slots_by, velocity, theta,
                a_sigma.reshape(1, owned), b_sigma.reshape(1, owned),
            ),
        )
    )
    across, total = lax.optimization_barrier((across, total))

    shards = (per_group // 2, members, owned)

    beyond = col_swap(across, 1)
    total, u_last, near_last, v_last = pl.pallas_call(
        middle_kernel,
        out_shape=[total_shape, *last_shapes, pltpu.VMEM(lowrank_v.shape[1:], BF16)],
        in_specs=[VMEM_SPEC] * 6 + [SMEM_SPEC] + [VMEM_SPEC] * 3 + [HBM_SPEC] * 3,
        out_specs=[VMEM_SPEC] * 4,
        scratch_shapes=[
            pltpu.VMEM((2, receivers, members, depth), BF16), pltpu.SemaphoreType.DMA((3,))
        ],
        input_output_aliases={7: 0, 8: 1, 9: 2},
        **params(4 * members * size, 4 * size),
    )(
        sibling, across, u_later, v_later, near_later, kept, slots, total, u_last, near_last,
        *map(in_hbm, weights),
    )
    total, swapped, same, other = pl.pallas_call(
        last_kernel,
        out_shape=[
            total_shape,
            pltpu.VMEM((3 * PACK // 2, members, LANES), BF16),
            *[pltpu.VMEM(shards, BF16)] * 2,
        ],
        in_specs=[VMEM_SPEC] * 5 + [SMEM_SPEC, VMEM_SPEC],
        out_specs=[VMEM_SPEC] * 4,
        scratch_shapes=[coeffs],
        input_output_aliases={6: 0},
        **params(2 * members * size, 2 * size),
    )(beyond, u_last, v_last, near_last, kept, slots, total)
    def send(value, by, bits, halves):
        pairs = []
        for i in range(groups * owners):
            col, row = divmod(i, owners)
            group, place = divmod(row, per_group)
            group = group ^ bits if col % 2 else (group + by) % n_groups
            place ^= per_group // 2 if halves[col % 2] else 0
            pairs.append((i, (col * n_groups + group) * per_group + place))
        return lax.ppermute(value, ("col", "row"), pairs)

    swapped = send(swapped, 0, 2, (True, False))
    other = send(other, 2, 3, (True, True))
    same = send(same, 2, 1, (False, True))
    own, first, second = pl.pallas_call(
        join_kernel,
        out_shape=[pltpu.VMEM(shards, dtype) for dtype in (F32, BF16, BF16)],
        in_specs=[VMEM_SPEC] * 2,
        out_specs=[VMEM_SPEC] * 3,
        **params(0, 8 * swapped.size),
    )(total, swapped)
    received = [
        other, same, send(first, 1, 0, (False, True)), send(second, 3, 1, (False, False))
    ]
    for place in reversed(range(per_group.bit_length() - 2)):
        shape = (own.shape[0] // 2, members, owned)
        sent, own = pl.pallas_call(
            functools.partial(halve_kernel, place),
            out_shape=[pltpu.VMEM(shape, F32)] * 2,
            in_specs=[VMEM_SPEC] * (1 + len(received)),
            out_specs=[VMEM_SPEC] * 2,
            **params(0, 12 * own.size),
        )(own, *received)
        received = [row_swap(sent, 1 << place)]
    stress_rate = own[0]
    for part in received:
        stress_rate = stress_rate + part[0, :members].astype(F32)
    return (stress_rate, stress_rate * gain + shift)


def solution(mesh):
    placed = (
        P(None, ("col", "row")),
        P(None, "row", "col"),
        P(None, "col", "row", None),
        P(None, "row", "col"),
        P(None, "row", "col"),
        P(None, "row", "col"),
        P(None, ("col", "row")),
        P(None, ("col", "row")),
        P(("col", "row")),
        P(("col", "row")),
    )
    return jax.shard_map(
        body,
        mesh=mesh,
        in_specs=placed,
        out_specs=(P(None, ("col", "row")), P(None, ("col", "row"))),
        check_vma=False,
    )
```
